32 devices in a mesh: dp: 8 (over y, x, core), mp: 4 (over z).
Axes of the slice: x: 2, y: 2, z: 4, core: 2. Of those that a mesh axis runs over, the one named last changes fastest.
Arguments:
- block_input: bfloat16 [16384, 1536], P('dp', 'mp'), may hold values from -6 to 6
- row_order: int32 [16, 1024], P('dp'), may hold values from 0 to 1023, as said below
- conv_weight: bfloat16 [5, 1536, 1536], P(None, 'mp'), may hold values from -0.0625 to 0.0625
- batch_gain: float32 [1536], P('mp'), may hold values from 0.25 to 1.75
- batch_bias: float32 [1536], P('mp'), may hold values from -1.75 to 1.75
- first_gain: float32 [1536], replicated, may hold values from 0.25 to 1.75
- first_bias: float32 [1536], replicated, may hold values from -1.75 to 1.75
- w_query: bfloat16 [1536, 512], P(None, 'mp'), may hold values from -0.15625 to 0.15625
- w_key: bfloat16 [1536, 512], P(None, 'mp'), may hold values from -0.15625 to 0.15625
- w_value: bfloat16 [1536, 1536], P(None, 'mp'), may hold values from -0.15625 to 0.15625
- relative_weight: bfloat16 [192, 512], P(None, 'mp'), may hold values from -0.4375 to 0.4375
- content_bias: float32 [8, 64], P('mp'), may hold values from -0.875 to 0.875
- position_bias: float32 [8, 64], P('mp'), may hold values from -0.875 to 0.875
- w_out: bfloat16 [1536, 1536], P('mp'), may hold values from -1.25 to 1.25
- second_gain: float32 [1536], replicated, may hold values from 0.25 to 1.75
- second_bias: float32 [1536], replicated, may hold values from -1.75 to 1.75
- w_inner: bfloat16 [1536, 3072], P(None, 'mp'), may hold values from -0.15625 to 0.15625
- inner_bias: float32 [3072], P('mp'), may hold values from -1.75 to 1.75
- w_outer: bfloat16 [3072, 1536], P('mp'), may hold values from -0.109375 to 0.109375
- cotangent: bfloat16 [16384, 1536], P('dp'), may hold values from -7 to 7
Outputs:
- block_output: bfloat16 [16384, 1536], P(('dp', 'mp'))
- grad_input: float32 [16384, 1536], P('dp', 'mp')
- grad_conv: float32 [5, 1536, 1536], P(None, 'mp')
- grad_batch_gain: float32 [1536], P('mp')
- grad_batch_bias: float32 [1536], P('mp')
- grad_first_gain: float32 [1536], replicated
- grad_first_bias: float32 [1536], replicated
- grad_query: float32 [1536, 512], P(None, 'mp')
- grad_key: float32 [1536, 512], P(None, 'mp')
- grad_value: float32 [1536, 1536], P(None, 'mp')
- grad_relative: float32 [192, 512], P(None, 'mp')
- grad_content_bias: float32 [8, 64], P('mp')
- grad_position_bias: float32 [8, 64], P('mp')
- grad_projection: float32 [1536, 1536], P('mp')
- grad_second_gain: float32 [1536], replicated
- grad_second_bias: float32 [1536], replicated
- grad_inner: float32 [1536, 3072], P(None, 'mp')
- grad_inner_bias: float32 [3072], P('mp')
- grad_outer: float32 [3072, 1536], P('mp')
The draws below stay inside these ranges and needn't reach their ends.
Inputs may be any that keep to these rules, and one draw needn't show every extreme that they name: `row_order`: each row holds every number of 0 to 1023 once: the positions cyclically shifted, and reversed in some rows.
All inputs are finite; a program needn't handle non-finite values.
Results may differ from the reference program's by a relative error of at most 0.01.
Values may be sent and summed in bfloat16 or wider, within the bound.
A program may use at most 256 MiB of HBM per device.

```python
import math
from functools import partial
import jax
import jax.numpy as jnp
from jax import lax

D = 1536
H = 8
DK = 64
DV = 192
RF = 192
FF = 3072
KW = 5
SEQUENCE_LENGTH = 1024
SEQS = 16
TOKENS = 16384
BLOCK = 512


def draw_row_order(key, part):
    key = jax.random.fold_in(key, 11)
    shift_key, flip_key = jax.random.split(key)
    shifts = jax.random.randint(shift_key, (SEQS, 1), 0, SEQUENCE_LENGTH)
    flips = jax.random.randint(flip_key, (SEQS, 1), 0, 2)
    onward = (jnp.arange(SEQUENCE_LENGTH, dtype=jnp.int32)[None, :] + shifts) % SEQUENCE_LENGTH
    return jnp.where(flips == 1, SEQUENCE_LENGTH - 1 - onward, onward).astype(jnp.int32)


def draw_cotangent(key, part):
    key = jax.random.fold_in(key, 23)
    noise_key, common_key = jax.random.split(key)
    noise = jnp.clip(jax.random.normal(noise_key, (TOKENS, D), jnp.float32), -6.0, 6.0)
    common = jnp.clip(0.3 * jax.random.normal(common_key, (D,), jnp.float32), -1.0, 1.0)
    return (noise + common[None, :]).astype(jnp.bfloat16)


def shard_levels(key, dims, cuts, low, top_value):
    level, own = 1.0, jax.random.fold_in(key, 6)
    for dim, parts in cuts:
        heights = jnp.exp(jax.random.uniform(jax.random.fold_in(own, dim), (parts,), jnp.float32, low / len(cuts), top_value / len(cuts)))
        level = level * jnp.repeat(heights, dims[dim] // parts).reshape([-1 if axis == dim else 1 for axis in range(len(dims))])
    return level


def normal_values(own_key, extent, scale, most, pieces=(), held_as=jnp.bfloat16):
    entries = scale * jax.random.normal(own_key, extent, jnp.float32)
    if pieces:
        entries = entries * shard_levels(own_key, extent, pieces, -0.22, 0.18)
    return jnp.clip(entries, -most, most).astype(held_as)


def setup_inputs(seed: int = 0) -> dict:
    splits = jax.random.split(jax.random.key(seed), 21)
    block_input = normal_values(splits[0], (TOKENS, D), 1.0, 6.0, ((0, 8), (1, 4)))
    row_order = draw_row_order(jax.random.fold_in(splits[20], 71), 0)
    conv_weight = normal_values(splits[2], (KW, D, D), (KW * D) ** -0.5, 0.0625, ((1, 4),))
    batch_gain = jnp.clip(1.0 + 0.15 * jax.random.normal(splits[3], (D,), jnp.float32), 0.25, 1.75)
    batch_bias = normal_values(splits[4], (D,), 0.3, 1.75, ((0, 4),), jnp.float32)
    first_gain = jnp.clip(1.0 + 0.15 * jax.random.normal(splits[5], (D,), jnp.float32), 0.25, 1.75)
    first_bias = normal_values(splits[6], (D,), 0.3, 1.75, (), jnp.float32)
    w_query = normal_values(splits[7], (D, H * DK), D ** -0.5, 0.15625, ((1, 4),))
    w_key = normal_values(splits[8], (D, H * DK), D ** -0.5, 0.15625, ((1, 4),))
    w_value = normal_values(splits[9], (D, H * DV), D ** -0.5, 0.15625, ((1, 4),))
    relative_weight = normal_values(splits[10], (RF, H * DK), RF ** -0.5, 0.4375, ((1, 4),))
    content_bias = normal_values(splits[11], (H, DK), 0.15, 0.875, ((0, 4),), jnp.float32)
    position_bias = normal_values(splits[12], (H, DK), 0.15, 0.875, ((0, 4),), jnp.float32)
    w_out = normal_values(splits[13], (H * DV, D), (max(8, H * DV * 16 // SEQUENCE_LENGTH)) ** -0.5, 1.25, ((0, 4),))
    second_gain = jnp.clip(1.0 + 0.15 * jax.random.normal(splits[14], (D,), jnp.float32), 0.25, 1.75)
    second_bias = normal_values(splits[15], (D,), 0.3, 1.75, (), jnp.float32)
    w_inner = normal_values(splits[16], (D, FF), D ** -0.5, 0.15625, ((1, 4),))
    inner_bias = normal_values(splits[17], (FF,), 0.3, 1.75, ((0, 4),), jnp.float32)
    w_outer = normal_values(splits[18], (FF, D), FF ** -0.5, 0.109375, ((0, 4),))
    cotangent = draw_cotangent(jax.random.fold_in(splits[20], 71), 0)
    return dict(block_input=block_input, row_order=row_order, conv_weight=conv_weight, batch_gain=batch_gain, batch_bias=batch_bias, first_gain=first_gain, first_bias=first_bias, w_query=w_query, w_key=w_key, w_value=w_value, relative_weight=relative_weight, content_bias=content_bias, position_bias=position_bias, w_out=w_out, second_gain=second_gain, second_bias=second_bias, w_inner=w_inner, inner_bias=inner_bias, w_outer=w_outer, cotangent=cotangent)


EPSILON = 1e-05
HIGH_PRECISION = lax.Precision.HIGHEST

@jax.custom_vjp
def low(v):
    return lax.optimization_barrier(v.astype(jnp.bfloat16)).astype(jnp.float32)

@jax.custom_vjp
def low_back(v):
    return v

def low_keep(v):
    return (low(v), None)

def low_pass(kept, grad):
    return (grad,)

def back_keep(v):
    return (v, None)

def back_low(kept, grad):
    return (low(grad),)
low.defvjp(low_keep, low_pass)
low_back.defvjp(back_keep, back_low)

def gelu(value):
    return value * jax.nn.sigmoid(1.702 * value)

def layer_norm(rows, gain, bias):
    centre = rows - lax.optimization_barrier(jnp.mean(rows, axis=-1, keepdims=True))
    spread = lax.optimization_barrier(jnp.mean(centre * centre, axis=-1, keepdims=True))
    return centre * lax.rsqrt(spread + EPSILON) * gain + bias

def relative_basis(length, features):
    distance = jnp.arange(2 * length - 1, dtype=jnp.float32) - (length - 1)
    half = features // 2
    ratio = jnp.arange(half, dtype=jnp.float32) / (half - 1)
    life = jnp.power(jnp.float32(length), ratio)
    decay = jnp.exp(-math.log(2.0) * jnp.abs(distance)[:, None] / life[None, :])
    return jnp.concatenate([decay, jnp.sign(distance)[:, None] * decay], axis=1)

def rel_shift(window, length):
    heads, rows, width = window.shape
    padded_input = jnp.pad(window, ((0, 0), (0, 0), (0, 1)))
    flat = padded_input.reshape(heads, rows * (width + 1))
    taken = flat[:, rows - 1:rows - 1 + rows * width]
    return taken.reshape(heads, rows, width)[:, :, :length]

def pick_rows(rows, order):
    return rows[order]

def attend_block(query_w, query_r, keys, values, rel_keys, first_row):
    block_w = lax.dynamic_slice_in_dim(query_w, first_row, BLOCK, 0)
    block_r = lax.dynamic_slice_in_dim(query_r, first_row, BLOCK, 0)
    window = lax.dynamic_slice_in_dim(rel_keys, (SEQUENCE_LENGTH - first_row - BLOCK).astype(jnp.int32), SEQUENCE_LENGTH + BLOCK - 1, 0)
    content = jnp.einsum('rhd,khd->hrk', block_w, keys, precision=HIGH_PRECISION)
    position = rel_shift(jnp.einsum('rhd,whd->hrw', block_r, window, precision=HIGH_PRECISION), SEQUENCE_LENGTH)
    logits = low_back(content + position)
    highest = lax.optimization_barrier(jnp.max(logits, axis=-1, keepdims=True))
    weights = jnp.exp(logits - highest)
    prob = low(weights / lax.optimization_barrier(jnp.sum(weights, axis=-1, keepdims=True)))
    return jnp.einsum('hrk,khd->rhd', prob, values, precision=HIGH_PRECISION)

def attend_sequence(rel_keys, operands):
    query_w, query_r, keys, values = operands
    starts = jnp.arange(SEQUENCE_LENGTH // BLOCK, dtype=jnp.int32) * BLOCK
    blocks = lax.map(jax.checkpoint(partial(attend_block, query_w, query_r, keys, values, rel_keys)), starts)
    return blocks.reshape(SEQUENCE_LENGTH, H, DV)

def reference(block_input, row_order, conv_weight, batch_gain, batch_bias, first_gain, first_bias, w_query, w_key, w_value, relative_weight, content_bias, position_bias, w_out, second_gain, second_bias, w_inner, inner_bias, w_outer, cotangent):
    params = (block_input, conv_weight, batch_gain, batch_bias, first_gain, first_bias, w_query, w_key, w_value, relative_weight, content_bias, position_bias, w_out, second_gain, second_bias, w_inner, inner_bias, w_outer)
    floats = tuple((item.astype(jnp.float32) for item in params))
    seq_total = block_input.shape[0] // SEQUENCE_LENGTH
    reach = KW // 2
    scale = DK ** (-0.5)

    def forward(source, convolution_taps, b_gain, b_bias, f_gain, f_bias, q_weight, k_weight, v_weight, r_weight, c_bias, p_bias, o_weight, s_gain, s_bias, i_weight, i_bias, u_weight):
        shifted = jax.vmap(pick_rows)(source.reshape(seq_total, SEQUENCE_LENGTH, D), row_order)
        batch_mean = lax.optimization_barrier(jnp.mean(shifted, axis=(0, 1)))
        batch_var = lax.optimization_barrier(jnp.mean(shifted * shifted, axis=(0, 1))) - batch_mean * batch_mean
        centred = (shifted - batch_mean) * lax.rsqrt(batch_var + EPSILON)
        act = low(gelu(b_gain * centred + b_bias))
        padded_input = jnp.pad(act, ((0, 0), (reach, reach), (0, 0)))
        convolution_block = jnp.zeros((seq_total, SEQUENCE_LENGTH, D), jnp.float32)
        for shift_amount in range(KW):
            convolution_block = convolution_block + jnp.einsum('muk,kn->mun', padded_input[:, shift_amount:shift_amount + SEQUENCE_LENGTH], convolution_taps[shift_amount], precision=HIGH_PRECISION)
        resid_one = low_back((shifted + convolution_block).reshape(seq_total * SEQUENCE_LENGTH, D))
        normed_one = low(layer_norm(resid_one, f_gain, f_bias))
        query = low_back(jnp.dot(normed_one, q_weight, precision=HIGH_PRECISION)).reshape(seq_total, SEQUENCE_LENGTH, H, DK) * scale
        query_w = low(query + c_bias)
        query_r = low(query + p_bias)
        keys = low(low_back(jnp.dot(normed_one, k_weight, precision=HIGH_PRECISION))).reshape(seq_total, SEQUENCE_LENGTH, H, DK)
        values = low(low_back(jnp.dot(normed_one, v_weight, precision=HIGH_PRECISION))).reshape(seq_total, SEQUENCE_LENGTH, H, DV)
        basis = low(relative_basis(SEQUENCE_LENGTH, RF))
        rel_keys = low(low_back(jnp.dot(basis, r_weight, precision=HIGH_PRECISION))).reshape(2 * SEQUENCE_LENGTH - 1, H, DK)
        mixed = lax.map(jax.checkpoint(partial(attend_sequence, rel_keys)), (query_w, query_r, keys, values))
        attended = low(low_back(mixed.reshape(seq_total * SEQUENCE_LENGTH, H * DV)))
        resid_two = resid_one + low_back(jnp.dot(attended, o_weight, precision=HIGH_PRECISION))
        normed_two = low(layer_norm(resid_two, s_gain, s_bias))
        inner = low_back(jnp.dot(normed_two, i_weight, precision=HIGH_PRECISION) + i_bias)
        hidden = low(gelu(inner))
        return resid_two + low_back(jnp.dot(hidden, u_weight, precision=HIGH_PRECISION))
    result, pullback = jax.vjp(forward, *floats)
    grads = pullback(cotangent.astype(jnp.float32))
    return (result.astype(jnp.bfloat16), grads[0], grads[1], grads[2], grads[3], grads[4], grads[5], grads[6], grads[7], grads[8], grads[9], grads[10], grads[11], grads[12], grads[13], grads[14], grads[15], grads[16], grads[17])
```

```python
import functools
import math

import jax
import jax.numpy as jnp
from jax import lax
from jax.experimental import pallas as pl
from jax.experimental.pallas import tpu as pltpu
from jax.sharding import PartitionSpec as P

EPSILON = 1e-05
f32 = jnp.float32
bf16 = jnp.bfloat16
AXES = ("dp", "mp")
MESH = pl.DeviceIdType.MESH
NT = (((1,), (1,)), ((), ()))
TN = (((0,), (0,)), ((), ()))
NN = (((1,), (0,)), ((), ()))


def dot(a, b, dims=NN):
    return lax.dot_general(a, b, dims, preferred_element_type=f32)


def gelu(value):
    return value * jax.nn.sigmoid(1.702 * value)


def gelu_slope(value):
    sig = jax.nn.sigmoid(1.702 * value)
    return sig + 1.702 * value * sig * (1.0 - sig)


def norm_rows(rows, gain, bias):
    centre = rows - jnp.mean(rows, axis=-1, keepdims=True)
    spread = jnp.mean(centre * centre, axis=-1, keepdims=True)
    inverse = lax.rsqrt(spread + EPSILON)
    unit = centre * inverse
    return (unit * gain + bias, unit, inverse)


def norm_back(grad, unit, inverse, gain):
    scaled = grad * gain
    return inverse * (
        scaled
        - jnp.mean(scaled, axis=-1, keepdims=True)
        - unit * jnp.mean(scaled * unit, axis=-1, keepdims=True)
    )


def relative_basis(length, features):
    distance = jnp.arange(2 * length, dtype=f32) - (length - 1)
    half = features // 2
    ratio = jnp.arange(half, dtype=f32) / (half - 1)
    life = jnp.power(jnp.float32(length), ratio)
    decay = jnp.exp(-math.log(2.0) * jnp.abs(distance)[:, None] / life[None, :])
    return jnp.concatenate([decay, jnp.sign(distance)[:, None] * decay], axis=1)


def attend_kernel(dk, dv, bq, qw_ref, qr_ref, kv_ref, rel_ref, out_ref, prob_ref):
    rows, length = qw_ref.shape[1], kv_ref.shape[1]
    width = length + bq
    pair = qw_ref.shape[2] // dk
    lane = lax.broadcasted_iota(jnp.int32, (bq, pair * dk), 1) // dk
    keys = kv_ref[0, :, : pair * dk]
    for b in range(rows // bq):
        at = slice(b * bq, (b + 1) * bq)
        lo = rows - (b + 1) * bq
        window = rel_ref[0, lo : lo + width, :]
        qw, qr = qw_ref[0, at, :], qr_ref[0, at, :]
        zero = jnp.zeros_like(qw)
        mixed = []
        for h in range(pair):
            content = dot(jnp.where(lane == h, qw, zero), keys, NT)
            place = dot(jnp.where(lane == h, qr, zero), window, NT)
            place = pltpu.roll(place, width - (bq - 1), 1, stride=1, stride_axis=0)
            logits = content + place[:, :length]
            weights = jnp.exp(logits - jnp.max(logits, axis=1, keepdims=True))
            prob = (weights * (1.0 / jnp.sum(weights, axis=1, keepdims=True))).astype(bf16)
            prob_ref[0, h, at, :] = prob
            values = kv_ref[0, :, pair * dk + h * dv : pair * dk + (h + 1) * dv]
            mixed.append(dot(prob, values).astype(bf16))
        out_ref[0, at, :] = jnp.concatenate(mixed, axis=1)


def block_spec(*shape):
    return pl.BlockSpec((1,) + shape, lambda g: (g,) + (0,) * len(shape))


def attend(qw, qr, kv, rel, dk, dv, bq):
    groups, rows, qcols = qw.shape
    length, kvcols = kv.shape[1:]
    pair = qcols // dk
    return pl.pallas_call(
        functools.partial(attend_kernel, dk, dv, bq),
        grid=(groups,),
        in_specs=[
            block_spec(rows, qcols),
            block_spec(rows, qcols),
            block_spec(length, kvcols),
            block_spec(rel.shape[1], qcols),
        ],
        out_specs=[block_spec(rows, pair * dv), block_spec(pair, rows, length)],
        out_shape=[
            jax.ShapeDtypeStruct((groups, rows, pair * dv), bf16),
            jax.ShapeDtypeStruct((groups, pair, rows, length), bf16),
        ],
        compiler_params=pltpu.CompilerParams(vmem_limit_bytes=50 << 20),
    )(qw, qr, kv, rel)


def attend_back_kernel(
    dk, dv, bq, scale, qw_ref, qr_ref, kv_ref, rel_ref, prob_ref, dmix_ref,
    dq_ref, sums_ref, dkv_ref, drel_ref, dkt, dvt, drt,
):
    rows, length = qw_ref.shape[1], kv_ref.shape[1]
    width = length + bq
    pair = qw_ref.shape[2] // dk
    qcols = pair * dk
    lane = lax.broadcasted_iota(jnp.int32, (bq, qcols), 1) // dk
    across = lax.broadcasted_iota(jnp.int32, (bq, bq), 0)
    across = across + lax.broadcasted_iota(jnp.int32, (bq, bq), 1)
    flip = jnp.where(across == bq - 1, 1.0, 0.0).astype(bf16)
    keys = kv_ref[0, :, :qcols]
    sums_w = jnp.zeros((1, qcols), f32)
    sums_r = jnp.zeros((1, qcols), f32)
    drt[...] = jnp.zeros_like(drt)
    for b in range(rows // bq):
        at = slice(b * bq, (b + 1) * bq)
        lo = rows - (b + 1) * bq
        window = rel_ref[0, lo : lo + width, :]
        qw, qr = qw_ref[0, at, :], qr_ref[0, at, :]
        zero = jnp.zeros_like(qw)
        qr_flip = dot(flip, qr).astype(bf16)
        dqw = jnp.zeros((bq, qcols), f32)
        dqr = jnp.zeros((bq, qcols), f32)
        for h in range(pair):
            prob = prob_ref[0, h, at, :]
            values = kv_ref[0, :, qcols + h * dv : qcols + (h + 1) * dv]
            dmix = dmix_ref[0, at, h * dv : (h + 1) * dv]
            prob32 = prob.astype(f32)
            part = dot(dmix, values, NT) * prob32
            d_logits = part - prob32 * jnp.sum(part, axis=1, keepdims=True)
            d_logits = d_logits.astype(bf16)
            turned = jnp.concatenate(
                [dot(flip, d_logits), jnp.zeros((bq, width - length), f32)], axis=1
            )
            d_window = pltpu.roll(turned, 0, 1, stride=1, stride_axis=0).astype(bf16)
            dqw = dqw + jnp.where(lane == h, dot(d_logits, keys), 0.0)
            dqr = dqr + jnp.where(lane == h, dot(d_window, window), 0.0)
            key_part = dot(jnp.where(lane == h, qw, zero), d_logits, TN)
            value_part = dot(dmix, prob, TN)
            if b == 0 and h == 0:
                dkt[...] = key_part
            else:
                dkt[...] += key_part
            if b == 0:
                dvt[h] = value_part
            else:
                dvt[h] += value_part
            drt[:, lo : lo + width] += dot(jnp.where(lane == h, qr_flip, zero), d_window, TN)
        high = dqr.astype(bf16)
        dqr = dot(flip, high) + dot(flip, (dqr - high.astype(f32)).astype(bf16))
        sums_w += jnp.sum(dqw, axis=0, keepdims=True)
        sums_r += jnp.sum(dqr, axis=0, keepdims=True)
        dq_ref[0, at, :] = ((dqw + dqr) * scale).astype(bf16)
    sums_ref[0] = jnp.concatenate([sums_w, sums_r, jnp.zeros((6, qcols), f32)], axis=0)
    dkv_ref[0, :, :qcols] = dkt[...].T.astype(bf16)
    for h in range(pair):
        dkv_ref[0, :, qcols + h * dv : qcols + (h + 1) * dv] = dvt[h].T.astype(bf16)
    drel_ref[0] = drt[...].T.astype(bf16)


def attend_back(qw, qr, kv, rel, prob, dmix, dk, dv, bq, scale):
    groups, rows, qcols = qw.shape
    length, kvcols = kv.shape[1:]
    pair = qcols // dk
    rels = rel.shape[1]
    return pl.pallas_call(
        functools.partial(attend_back_kernel, dk, dv, bq, scale),
        grid=(groups,),
        in_specs=[
            block_spec(rows, qcols),
            block_spec(rows, qcols),
            block_spec(length, kvcols),
            block_spec(rels, qcols),
            block_spec(pair, rows, length),
            block_spec(rows, pair * dv),
        ],
        out_specs=[
            block_spec(rows, qcols),
            block_spec(8, qcols),
            block_spec(length, kvcols),
            block_spec(rels, qcols),
        ],
        out_shape=[
            jax.ShapeDtypeStruct((groups, rows, qcols), bf16),
            jax.ShapeDtypeStruct((groups, 8, qcols), f32),
            jax.ShapeDtypeStruct((groups, length, kvcols), bf16),
            jax.ShapeDtypeStruct((groups, rels, qcols), bf16),
        ],
        scratch_shapes=[
            pltpu.VMEM((qcols, length), f32),
            pltpu.VMEM((pair, dv, length), f32),
            pltpu.VMEM((qcols, rels), f32),
        ],
        compiler_params=pltpu.CompilerParams(vmem_limit_bytes=50 << 20),
    )(qw, qr, kv, rel, prob, dmix)


def line_of():
    core, level = lax.axis_index("dp") % 2, lax.axis_index("mp")
    depth = lax.axis_size("mp")
    rank = jnp.where(core == 0, level, depth - 1 - level)
    step = jnp.where(core == 0, 1, -1)
    place = lax.axis_index("dp")
    up, down, sibling = (place, level + step), (place, level - step), (place + 1 - 2 * core, level)
    return core, level, rank, up, down, sibling


def remote(src, dst, send_sem, recv_sem, device):
    return pltpu.make_async_remote_copy(
        src_ref=src,
        dst_ref=dst,
        send_sem=send_sem,
        recv_sem=recv_sem,
        device_id=device,
        device_id_type=MESH,
    )


def greet(rank, last, up, down, mates):
    barrier = pltpu.get_barrier_semaphore()

    @pl.when(rank < last)
    def _():
        pl.semaphore_signal(barrier, inc=1, device_id=up, device_id_type=MESH)

    @pl.when(rank > 0)
    def _():
        pl.semaphore_signal(barrier, inc=1, device_id=down, device_id_type=MESH)

    for mate in mates:
        pl.semaphore_signal(barrier, inc=1, device_id=mate, device_id_type=MESH)
    ends = (rank == 0) | (rank == last)
    pl.semaphore_wait(barrier, jnp.where(ends, 1 + len(mates), 2 + len(mates)))


def mate_of(place, level, bit):
    return place + (1 << bit) - (2 << bit) * (place // (1 << bit) % 2), level


class Both:
    def __init__(self, *copies):
        self.copies = copies

    def start(self):
        for copy in self.copies:
            copy.start()

    def wait_recv(self):
        for copy in self.copies:
            copy.wait_recv()

    def wait_send(self):
        for copy in self.copies:
            copy.wait_send()


def diagonal(size):
    row = lax.broadcasted_iota(jnp.int32, (1, size, size), 1)
    return jnp.where(row == lax.broadcasted_iota(jnp.int32, (1, size, size), 2), 1.0, 0.0)


def encode(rows, whole_ref, step_ref):
    step = jnp.max(jnp.abs(rows), axis=1, keepdims=True) * (1.0 / 32000.0)
    scaled = jnp.round(rows * (1.0 / jnp.maximum(step, 1e-30)))
    whole_ref[...] = scaled.astype(jnp.int32).astype(jnp.int16)
    step = step.reshape(rows.shape[0] // 128, 128, 1)
    step_ref[: step.shape[0], :] = jnp.sum(step * diagonal(128), axis=1)


def decode(whole_ref, step_ref):
    count = whole_ref.shape[0]
    step = step_ref[: count // 128, :].reshape(count // 128, 1, 128)
    step = jnp.sum(step * diagonal(128), axis=2, keepdims=True).reshape(count, 1)
    return whole_ref[...].astype(jnp.int32).astype(f32) * step


def front_kernel(
    chunk, taps, bits, total_rows,
    rows_ref, gain_ref, bias_ref, w_ref, share_ref, small_ref, cot_ref,
    resid_ref, act_ref, stats_ref, small_out, cot_out, weights_ref,
    acc, rx_far, rx_near, rx_back, tx_far, tx_near, stage, rx_half, tx_stats, rx_stats,
    rx_far_step, rx_near_step, rx_back_step, tx_far_step, tx_near_step,
    far_send, far_recv, near_send, near_recv, back_recv, swap_send, swap_recv,
    step_send, step_recv,
    stats_send, stats_recv, small_send, small_recv, cot_send, cot_recv, own_sem,
    up_send, down_send, level_recv, plane_send, plane_recv, cross_send, cross_recv,
    core_send, core_recv,
):
    core, level, rank, up, down, sibling = line_of()
    place = lax.axis_index("dp")
    levels = lax.axis_size("mp")
    own = place % 8
    seqs, length, own_cols = rows_ref.shape
    width = w_ref.shape[1]
    half = length // 2
    reach = taps // 2
    count = length // chunk
    per_half = count // 2
    tile = min(512, width)
    cut = width // 2
    mates = [mate_of(place, level, bit) for bit in range(bits)]

    barrier = pltpu.get_barrier_semaphore()
    for r in range(1, 4):
        other = (place, (level + r) % levels)
        pl.semaphore_signal(barrier, inc=1, device_id=other, device_id_type=MESH)
    for mate in mates:
        pl.semaphore_signal(barrier, inc=1, device_id=mate, device_id_type=MESH)

    values = rows_ref[...].astype(f32).reshape(seqs * length, own_cols)
    sums = jnp.sum(values, axis=0, keepdims=True)
    squares = jnp.sum(values * values, axis=0, keepdims=True)
    sums = jnp.concatenate([sums, squares, jnp.zeros((6, own_cols), f32)], axis=0)
    pl.semaphore_wait(barrier, 3 + bits)

    x_mate, y_mate = mates[1], mates[2]
    cross = [own + 2 - 4 * (own // 2 % 2), own + 4 - 8 * (own // 4)]
    corner = cross[0] + cross[1] - own
    left_half, right_half = slice(0, cut), slice(cut, width)

    def piece_at(q):
        base = jnp.where((level == 0) | (level == 3), q, jnp.where(q == 0, 1, jnp.where(q == 1, 0, q)))
        return jnp.where(level < 2, base, 3 - base)

    share_rows = share_ref.shape[0]

    def piece(z, block):
        return weights_ref.at[z, pl.ds(pl.multiple_of(block * share_rows, 16), share_rows)]

    def send(part, sems, device):
        return remote(part, part, sems[0], sems[1], device)

    def up_copy(z):
        return send(piece(z, own), (up_send.at[z], level_recv.at[z]), (place, level + 1))

    def down_copy(z):
        return send(piece(z, own), (down_send.at[z], level_recv.at[z]), (place, level - 1))

    def plane_copy(z, k):
        sems = (plane_send.at[z, k], plane_recv.at[z, k])
        return send(piece(z, own), sems, (x_mate, y_mate)[k])

    def cross_copy(z, k):
        part = piece(z, cross[1 - k]).at[:, (left_half, right_half)[k]]
        return send(part, (cross_send.at[z, k], cross_recv.at[z, k]), (x_mate, y_mate)[k])

    def core_copy(z, k):
        part = piece(z, (own, cross[0], cross[1], corner)[k])
        return send(part, (core_send.at[z, k], core_recv.at[z, k]), sibling)

    def weights_first(q):
        z = piece_at(q)

        @pl.when(z != level)
        def _():
            up_copy(z).wait_recv()

        @pl.when((z <= level) & (level < 3))
        def _():
            up_copy(z).start()

        @pl.when((z >= level) & (level > 0))
        def _():
            down_copy(z).start()

        plane_copy(z, 0).start()
        plane_copy(z, 1).start()
        core_copy(z, 0).start()

    def weights_second(q):
        z = piece_at(q)
        plane_copy(z, 0).wait_recv()
        plane_copy(z, 1).wait_recv()
        cross_copy(z, 0).start()
        cross_copy(z, 1).start()
        core_copy(z, 1).start()
        core_copy(z, 2).start()

    def weights_third(q):
        z = piece_at(q)
        cross_copy(z, 0).wait_recv()
        cross_copy(z, 1).wait_recv()
        core_copy(z, 3).start()

    def weights_fourth(q):
        z = piece_at(q)
        for k in range(4):
            core_copy(z, k).wait_recv()

    def weights_slot(t):
        for lag, part in enumerate((weights_first, weights_second, weights_third, weights_fourth)):
            if isinstance(t, int):
                if lag <= t < 4 + lag:
                    part(t - lag)
                continue

            @pl.when((t >= lag) & (t < 4 + lag))
            def _(lag=lag, part=part):
                part(t - lag)

    own_copy = pltpu.make_async_copy(share_ref, piece(level, own), own_sem)
    own_copy.start()

    def small_copy(r):
        other = (place, (level + r) % levels)
        sems = (small_send.at[r - 1], small_recv.at[level])
        return remote(small_ref, small_out.at[level], sems[0], sems[1], other)

    for r in range(1, 4):
        small_copy(r).start()
    small_out[level] = small_ref[...]
    cot_copy = remote(cot_ref.at[level % 2, 1 - core], cot_out, cot_send, cot_recv, sibling)
    cot_keep = pltpu.make_async_copy(cot_ref.at[level % 2, core], cot_out, cot_recv)

    @pl.when(rank < 2)
    def _():
        cot_copy.start()
        cot_keep.start()

    own_copy.wait()

    for bit in range(bits):
        tx_stats[bit] = sums
        copy = remote(
            tx_stats.at[bit], rx_stats.at[bit], stats_send.at[bit], stats_recv.at[bit], mates[bit]
        )
        copy.start()
        copy.wait()
        sums = sums + rx_stats[bit]
    weights_slot(0)
    mean = sums[0:1] / total_rows
    scale = lax.rsqrt(sums[1:2] / total_rows - mean * mean + EPSILON)
    stats_ref[...] = jnp.concatenate([mean, scale, jnp.zeros((6, own_cols), f32)], axis=0)
    row = lax.broadcasted_iota(jnp.int32, (length, own_cols), 0)
    for seq in range(seqs):
        centred = (rows_ref[seq].astype(f32) - mean) * scale
        act = gelu(gain_ref[...] * centred + bias_ref[...])
        for t in range(taps):
            moved = pltpu.roll(act, (reach - t) % length, 0) if t != reach else act
            inside = (row + (t - reach) >= 0) & (row + (t - reach) < length)
            act_ref[seq, :, t * own_cols : (t + 1) * own_cols] = jnp.where(
                inside, moved, 0.0
            ).astype(bf16)

    def line_copy(c, whole, step, sems, k, device):
        rows = pl.ds(pl.multiple_of(c * chunk, chunk), chunk)
        return Both(
            remote(whole[0].at[rows], whole[1].at[rows], sems[0].at[c], sems[1].at[c], device),
            remote(
                step[0].at[c], step[1].at[c], step_send.at[min(k, 1), c], step_recv.at[k, c], device
            ),
        )

    def far_copy(c):
        step = (tx_far_step, rx_far_step)
        return line_copy(c, (tx_far, rx_far), step, (far_send, far_recv), 0, down)

    def near_copy(c):
        step = (tx_near_step, rx_near_step)
        return line_copy(c, (tx_near, rx_near), step, (near_send, near_recv), 1, down)

    def back_copy(c):
        step = (tx_near_step, rx_back_step)
        return line_copy(c, (tx_near, rx_back), step, (near_send, back_recv), 2, up)

    def swap_copy(h):
        rows = pl.ds(h * chunk, chunk)
        return remote(stage.at[rows], rx_half.at[rows], swap_send.at[h], swap_recv.at[h], sibling)

    def finish(c):
        rows = pl.ds(c % per_half * chunk, chunk)

        @pl.when(c // per_half == core)
        def _():
            resid_ref[rows, :] = acc[...]

        @pl.when(c // per_half != core)
        def _():
            stage[rows, :] = acc[...]
            swap_copy(c % per_half).start()

    def step(i, _):
        @pl.when((rank == 0) & (i >= count))
        def _():
            weights_slot(i - count + 1)

        @pl.when(((rank == 1) | (rank == 2)) & (i % 2 == 1))
        def _():
            weights_slot(i // 2 + 1)

        c = i % count
        near = jnp.where(rank == 0, i < count, i >= count)
        seq = jnp.where(near, 1, 0)
        rows = pl.ds(pl.multiple_of(c * chunk, chunk), chunk)
        for n in range(width // tile):
            cols = slice(n * tile, (n + 1) * tile)
            acc[:, cols] = dot(act_ref[seq, rows, :], w_ref[:, cols])
        here = pl.ds(pl.multiple_of(level * own_cols, 128), own_cols)
        acc[:, here] += rows_ref[seq, rows, :].astype(f32)

        @pl.when(jnp.logical_not(near))
        def _():
            @pl.when(rank < 3)
            def _():
                far_copy(c).wait_recv()
                acc[...] += decode(rx_far.at[rows], rx_far_step.at[c])

            @pl.when(rank > 0)
            def _():
                encode(acc[...], tx_far.at[rows], tx_far_step.at[c])

                @pl.when(c >= 2)
                def _():
                    far_copy(c - 2).wait_send()

                far_copy(c).start()

            @pl.when(rank == 0)
            def _():
                finish(c)

                @pl.when(c >= 1)
                def _():
                    back_copy(c - 1).wait_send()

                back_copy(c).start()

        @pl.when(near)
        def _():
            @pl.when((rank == 1) | (rank == 2))
            def _():
                near_copy(c).wait_recv()
                acc[...] += decode(rx_near.at[rows], rx_near_step.at[c])

            @pl.when(rank == 1)
            def _():
                back_copy(c).wait_recv()
                acc[...] += decode(rx_back.at[rows], rx_back_step.at[c])
                finish(c)

            @pl.when(rank != 1)
            def _():
                encode(acc[...], tx_near.at[rows], tx_near_step.at[c])

            @pl.when(rank >= 2)
            def _():
                @pl.when(c < 2)
                def _():
                    far_copy(count - 2 + c).wait_send()

                @pl.when(c >= 2)
                def _():
                    near_copy(c - 2).wait_send()

                near_copy(c).start()

        return 0

    lax.fori_loop(0, 2 * count, step, 0)
    @pl.when(rank == 3)
    def _():
        lax.fori_loop(1, count + 1, lambda t, _: (weights_slot(t), 0)[1], 0)

    for t in range(count + 1, 7):
        weights_slot(t)

    @pl.when(rank >= 2)
    def _():
        def take(h, _):
            rows = pl.ds(pl.multiple_of(h * chunk, chunk), chunk)
            swap_copy(h).wait_recv()
            resid_ref[rows, :] = rx_half[rows, :]
            return 0

        lax.fori_loop(0, per_half, take, 0)
        cot_copy.wait_recv()

    @pl.when(rank < 2)
    def _():
        lax.fori_loop(0, per_half, lambda h, _: (swap_copy(h).wait_send(), 0)[1], 0)
        cot_copy.wait_send()
        cot_keep.wait()

    @pl.when(rank == 1)
    def _():
        far_copy(count - 2).wait_send()
        far_copy(count - 1).wait_send()

    @pl.when(rank >= 2)
    def _():
        near_copy(count - 2).wait_send()
        near_copy(count - 1).wait_send()

    @pl.when(rank == 0)
    def _():
        back_copy(count - 1).wait_send()

    for r in range(1, 4):
        small_copy(r).wait_send()
        other = (level + r) % levels
        part = small_out.at[other]
        remote(part, part, small_send.at[r - 1], small_recv.at[other], sibling).wait_recv()

    def end(z, _):
        @pl.when((z <= level) & (level < 3))
        def _():
            up_copy(z).wait_send()

        @pl.when((z >= level) & (level > 0))
        def _():
            down_copy(z).wait_send()

        for k in range(2):
            plane_copy(z, k).wait_send()
            cross_copy(z, k).wait_send()
        for k in range(4):
            core_copy(z, k).wait_send()
        return 0

    lax.fori_loop(0, levels, end, 0)


def whole_spec():
    return pl.BlockSpec(memory_space=pltpu.VMEM)


def any_spec():
    return pl.BlockSpec(memory_space=pl.ANY)


def front(rows, gain, bias, weight, share, small, cot, taps, bits, total_rows, chunk):
    seqs, length, own_cols = rows.shape
    depth, width = weight.shape
    levels = lax.axis_size("mp")
    half, count = length // 2, length // chunk
    dma = pltpu.SemaphoreType.DMA
    shape = jax.ShapeDtypeStruct
    return pl.pallas_call(
        functools.partial(front_kernel, chunk, taps, bits, total_rows),
        in_specs=[whole_spec()] * 6 + [any_spec()],
        out_specs=[whole_spec()] * 5 + [any_spec()],
        out_shape=[
            shape((half, width), f32),
            shape((seqs, length, depth), bf16),
            shape((8, own_cols), f32),
            shape((levels,) + small.shape, f32),
            shape((half, width), bf16),
            shape((levels, 8 * share.shape[0], width), bf16),
        ],
        scratch_shapes=[
            pltpu.VMEM((chunk, width), f32),
            pltpu.VMEM((length, width), jnp.int16),
            pltpu.VMEM((length, width), jnp.int16),
            pltpu.VMEM((length, width), jnp.int16),
            pltpu.VMEM((length, width), jnp.int16),
            pltpu.VMEM((length, width), jnp.int16),
            pltpu.VMEM((half, width), f32),
            pltpu.VMEM((half, width), f32),
            pltpu.VMEM((bits, 8, own_cols), f32),
            pltpu.VMEM((bits, 8, own_cols), f32),
            pltpu.VMEM((count, 8, 128), f32),
            pltpu.VMEM((count, 8, 128), f32),
            pltpu.VMEM((count, 8, 128), f32),
            pltpu.VMEM((count, 8, 128), f32),
            pltpu.VMEM((count, 8, 128), f32),
            dma((count,)),
            dma((count,)),
            dma((count,)),
            dma((count,)),
            dma((count,)),
            dma((count // 2,)),
            dma((count // 2,)),
            dma((2, count)),
            dma((3, count)),
            dma((bits,)),
            dma((bits,)),
            dma((3,)),
            dma((levels,)),
            dma(()),
            dma(()),
            dma(()),
            dma((levels,)),
            dma((levels,)),
            dma((levels,)),
            dma((levels, 2)),
            dma((levels, 2)),
            dma((levels, 2)),
            dma((levels, 2)),
            dma((levels, 4)),
            dma((levels, 4)),
        ],
        cost_estimate=pl.CostEstimate(
            flops=4 * length * depth * width, bytes_accessed=400 << 20, transcendentals=0
        ),
        compiler_params=pltpu.CompilerParams(
            collective_id=0, has_side_effects=True, vmem_limit_bytes=56 << 20
        ),
    )(rows, gain, bias, weight, share, small, cot)


def conv_back_kernel(
    chunk, taps, grad_ref, act_ref, w_ref, other_ref, dact_ref, dcol_ref, gw_ref, part_ref, rx_one,
    whole, gsum, acc, own_sum, loaded, rx_two, rx_three,
    half_send, half_recv, far_send, far_recv, near_send, near_recv, back_send, back_recv,
    keep_sem, out_sem, own_sem, load_sem, one_send, one_recv, two_send, two_recv, three_send, three_recv,
):
    core, level, rank, up, down, sibling = line_of()
    length, width = whole.shape[1:]
    half = length // 2
    own_cols = dcol_ref.shape[2]
    count = length // chunk
    reach = taps // 2
    tile = min(512, width)
    place = lax.axis_index("dp")
    x_mate, y_mate = mate_of(place, level, 1), mate_of(place, level, 2)
    b0, b1, b2 = place % 2, place // 2 % 2, place // 4 % 2
    levels = other_ref.shape[3]
    cut = width // 2
    left_half, right_half = slice(0, cut), slice(cut, width)
    greet(rank, 3, up, down, (sibling, x_mate, y_mate))

    def own_load(z):
        return pltpu.make_async_copy(other_ref.at[:, :, b0, z], own_sum.at[z], own_sem.at[z])

    def one_copy(z):
        part = other_ref.at[:, :, 1 - b0, z]
        return remote(part, rx_one.at[z], one_send.at[z], one_recv.at[z], sibling)

    def two_copy(z, k):
        if k == 0:
            part = own_sum.at[z, :, 1 - b1, :, left_half]
        else:
            part = own_sum.at[z, 1 - b2, :, :, right_half]
        sems = (two_send.at[z, k], two_recv.at[z, k])
        return remote(part, rx_two.at[z, k], sems[0], sems[1], (x_mate, y_mate)[k])

    def three_copy(z, k):
        if k == 0:
            part = own_sum.at[z, 1 - b2, b1, :, left_half]
        else:
            part = own_sum.at[z, b2, 1 - b1, :, right_half]
        sems = (three_send.at[z, k], three_recv.at[z, k])
        return remote(part, rx_three.at[z, k], sems[0], sems[1], (y_mate, x_mate)[k])

    def added(left, right):
        return (left.astype(f32) + right.astype(f32)).astype(bf16)

    def other_second(z):
        one_copy(z).wait_recv()
        load = pltpu.make_async_copy(rx_one.at[z], loaded, load_sem)
        load.start()
        own_load(z).wait()
        load.wait()
        own_sum[z] = added(own_sum[z], loaded[...])
        two_copy(z, 0).start()
        two_copy(z, 1).start()

    def other_third(z):
        two_copy(z, 0).wait_recv()
        two_copy(z, 1).wait_recv()
        for b in range(2):
            kept = own_sum[z, b, b1, :, left_half]
            own_sum[z, b, b1, :, left_half] = added(kept, rx_two[z, 0, b])
            kept = own_sum[z, b2, b, :, right_half]
            own_sum[z, b2, b, :, right_half] = added(kept, rx_two[z, 1, b])
        three_copy(z, 0).start()
        three_copy(z, 1).start()

    def other_fourth(z):
        three_copy(z, 0).wait_recv()
        three_copy(z, 1).wait_recv()
        part_ref[z, :, left_half] = added(own_sum[z, b2, b1, :, left_half], rx_three[z, 0])
        part_ref[z, :, right_half] = added(own_sum[z, b2, b1, :, right_half], rx_three[z, 1])

    def far_copy(c):
        rows = pl.ds(c * chunk, chunk)
        part = whole.at[0, rows]
        return remote(part, part, far_send.at[c], far_recv.at[c], up)

    def near_copy(c):
        rows = pl.ds(c * chunk, chunk)
        part = whole.at[1, rows]
        return remote(part, part, near_send.at[c], near_recv.at[c], up)

    def back_copy(c):
        rows = pl.ds(c * chunk, chunk)
        part = whole.at[1, rows]
        return remote(part, part, back_send.at[c], back_recv.at[c], down)

    slot = jnp.where((rank == 0) | (rank == 3), 0, 1)
    mine = whole.at[slot, pl.ds(core * half, half)]
    half_copy = remote(grad_ref, mine, half_send, half_recv, sibling)
    keep_copy = pltpu.make_async_copy(grad_ref, mine, keep_sem)

    @pl.when(rank >= 2)
    def _():
        half_copy.start()

    @pl.when(rank < 2)
    def _():
        keep_copy.start()

    for z in range(levels):
        one_copy(z).start()
        own_load(z).start()
    gsum[...] = jnp.zeros_like(gsum)
    acc[...] = jnp.zeros_like(acc)

    @pl.when(rank >= 2)
    def _():
        half_copy.wait_send()

    @pl.when(rank < 2)
    def _():
        keep_copy.wait()
        half_copy.wait_recv()

    def item(i):
        edge = (i == 0) | (i == 2 * count - 1)
        near = (i == 0) | ((i % 2 == 1) & (i != 2 * count - 1))
        c = jnp.where(edge, jnp.where(near, 0, count - 1), jnp.where(near, (i + 1) // 2, i // 2 - 1))
        return jnp.where(rank == 0, i >= count, near), jnp.where(rank == 0, i % count, c)

    def sent(i):
        near, c = item(i)

        @pl.when(near)
        def _():
            near_copy(c).wait_send()

        @pl.when(jnp.logical_not(near))
        def _():
            far_copy(c).wait_send()

    def step(i, _):
        @pl.when((i >= 1) & (i < 1 + levels))
        def _():
            other_second(i - 1)

        @pl.when((i >= 3) & (i < 3 + levels))
        def _():
            other_third(i - 3)

        @pl.when(i >= 5)
        def _():
            other_fourth(i - 5)

        near, c = item(i)
        seq = jnp.where(near, 1, 0)

        @pl.when(near)
        def _():
            @pl.when(rank >= 2)
            def _():
                near_copy(c).wait_recv()

            @pl.when(rank == 0)
            def _():
                back_copy(c).wait_recv()

        @pl.when(jnp.logical_not(near) & (rank > 0))
        def _():
            far_copy(c).wait_recv()

        @pl.when(((rank == 1) | (rank == 2)) & (i >= 2) | (rank == 0) & (i >= 2) & (i < count))
        def _():
            sent(i - 2)

        @pl.when(near & ((rank == 1) | (rank == 2)))
        def _():
            near_copy(c).start()

        @pl.when(near & (rank == 1))
        def _():
            @pl.when(c >= 2)
            def _():
                back_copy(c - 2).wait_send()

            back_copy(c).start()

        @pl.when(jnp.logical_not(near) & (rank < 3))
        def _():
            far_copy(c).start()

        rows = pl.ds(pl.multiple_of(c * chunk, chunk), chunk)
        grad = whole[seq, rows, :]
        own = pl.ds(pl.multiple_of(level * own_cols, 128), own_cols)
        dcol_ref[seq, rows, :] = whole[seq, rows, own]
        edge_rows = jnp.zeros((8, own_cols), f32)
        total = jnp.zeros((chunk + 16, own_cols), f32)
        for t in range(taps):
            term = dot(grad, w_ref[t * own_cols : (t + 1) * own_cols, :], NT)
            term = jnp.concatenate([edge_rows, term, edge_rows], axis=0)
            total = total + pltpu.roll(term, (t - reach) % (chunk + 16), 0)
        acc[seq, pl.ds(pl.multiple_of(c * chunk, 8), chunk + 16), :] += total
        for t in range(taps):
            left = act_ref[seq, rows, t * own_cols : (t + 1) * own_cols]
            for n in range(width // tile):
                cols = slice(n * tile, (n + 1) * tile)
                gsum[t * own_cols : (t + 1) * own_cols, cols] += dot(left, grad[:, cols], TN)
        return 0

    lax.fori_loop(0, 2 * count, step, 0)
    for z in range(2 * count - 5, levels):
        other_fourth(z)
    dact_out = pltpu.make_async_copy(acc.at[:, 8 : 8 + length], dact_ref, out_sem.at[0])
    dact_out.start()

    @pl.when(rank == 0)
    def _():
        sent(count - 2)
        sent(count - 1)

    @pl.when((rank == 1) | (rank == 2))
    def _():
        sent(2 * count - 2)
        sent(2 * count - 1)

    @pl.when(rank == 1)
    def _():
        back_copy(count - 2).wait_send()
        back_copy(count - 1).wait_send()

    for n in range(2):
        size = min(length, gsum.shape[0] - n * length)
        whole[n, :size] = gsum[n * length : n * length + size].astype(bf16)
        out = pltpu.make_async_copy(
            whole.at[n, :size], gw_ref.at[n * length : n * length + size], out_sem.at[1 + n]
        )
        out.start()
    for z in range(levels):
        one_copy(z).wait_send()
        for k in range(2):
            two_copy(z, k).wait_send()
            three_copy(z, k).wait_send()
    dact_out.wait()
    for n in range(2):
        size = min(length, gsum.shape[0] - n * length)
        pltpu.make_async_copy(
            whole.at[n, :size], gw_ref.at[n * length : n * length + size], out_sem.at[1 + n]
        ).wait()


def conv_back(grad, act_taps, weight, other, taps, chunk):
    seqs, length, depth = act_taps.shape
    width = weight.shape[1]
    own_cols = depth // taps
    count = length // chunk
    cell, levels, share, _ = other.shape
    dma = pltpu.SemaphoreType.DMA
    shape = jax.ShapeDtypeStruct
    return pl.pallas_call(
        functools.partial(conv_back_kernel, chunk, taps),
        in_specs=[any_spec(), whole_spec(), whole_spec(), any_spec()],
        out_specs=[any_spec(), whole_spec(), any_spec(), whole_spec(), any_spec()],
        out_shape=[
            shape((seqs, length, own_cols), f32),
            shape((seqs, length, own_cols), bf16),
            shape((depth, width), bf16),
            shape((levels, share, width), bf16),
            shape((levels, 2, 2, share, width), bf16),
        ],
        scratch_shapes=[
            pltpu.VMEM((seqs, length, width), bf16),
            pltpu.VMEM((depth, width), f32),
            pltpu.VMEM((seqs, length + 16, own_cols), f32),
            pltpu.VMEM((levels, 2, 2, share, width), bf16),
            pltpu.VMEM((2, 2, share, width), bf16),
            pltpu.VMEM((levels, 2, 2, share, width // 2), bf16),
            pltpu.VMEM((levels, 2, share, width // 2), bf16),
            dma(()),
            dma(()),
            dma((count,)),
            dma((count,)),
            dma((count,)),
            dma((count,)),
            dma((count,)),
            dma((count,)),
            dma(()),
            dma((3,)),
            dma((levels,)),
            dma(()),
            dma((levels,)),
            dma((levels,)),
            dma((levels, 2)),
            dma((levels, 2)),
            dma((levels, 2)),
            dma((levels, 2)),
        ],
        compiler_params=pltpu.CompilerParams(
            collective_id=1, has_side_effects=True, vmem_limit_bytes=58 << 20
        ),
    )(grad, act_taps, weight, other.reshape(2, 2, 2, levels, share, width))


def weight_grads_kernel(cell, count, *refs):
    out_ref, total = refs[-2], refs[-1]
    at = 0
    for i in range(count):
        left_ref, right_ref = refs[2 * i], refs[2 * i + 1]
        cols = left_ref.shape[2]
        tile = 256 if cols % 256 == 0 else 128
        for n in range(cols // tile):
            part = slice(n * tile, (n + 1) * tile)
            total[part, :] = dot(left_ref[0, :, part], right_ref[...], TN)
        rows = cols // cell
        for p in range(cell):
            out_ref[p, 0, at : at + rows, :] = total[p * rows : (p + 1) * rows, :].astype(bf16)
        at += rows
    if len(refs) > 2 * count + 2:
        extra_ref = refs[2 * count]
        out_ref[:, 0, at:, :] = extra_ref[:, 0]


def weight_grads(pairs, extra, cell):
    groups = pairs[0][0].shape[0]
    width = pairs[0][1].shape[1]
    rows = sum(left.shape[2] for left, _ in pairs) // cell
    specs, args = [], []
    for left, right in pairs:
        specs += [block_spec(*left.shape[1:]), pl.BlockSpec(right.shape, lambda g: (0, 0))]
        args += [left, right]
    if extra is not None:
        rows += extra.shape[2]
        specs.append(pl.BlockSpec((cell, 1) + extra.shape[2:], lambda g: (0, g, 0, 0)))
        args.append(extra)
    flops = sum(2 * left.size * width for left, _ in pairs)
    return pl.pallas_call(
        functools.partial(weight_grads_kernel, cell, len(pairs)),
        grid=(groups,),
        in_specs=specs,
        out_specs=pl.BlockSpec((cell, 1, rows, width), lambda g: (0, g, 0, 0)),
        out_shape=jax.ShapeDtypeStruct((cell, groups, rows, width), bf16),
        scratch_shapes=[pltpu.VMEM((max(left.shape[2] for left, _ in pairs), width), f32)],
        cost_estimate=pl.CostEstimate(flops=flops, bytes_accessed=30 << 20, transcendentals=0),
        compiler_params=pltpu.CompilerParams(vmem_limit_bytes=50 << 20),
    )(*args)


def last_sums_kernel(
    conv_ref, part_ref, conv_out, whole_out,
    total, rx_core, rx_two, tx_two, rx_three, tx_three, tx_line, rx_line,
    core_send, core_recv, two_send, two_recv, three_send, three_recv,
    back_send, back_recv, right_send, right_recv, left_send, left_recv, gather_send, gather_recv,
):
    place, level = lax.axis_index("dp"), lax.axis_index("mp")
    last = lax.axis_size("mp") - 1
    b0, b1, b2 = place % 2, place // 2 % 2, place // 4 % 2
    own = place % 8
    mates = [
        (place + 1 - 2 * b0, level),
        (place + 2 - 4 * b1, level),
        (place + 4 - 8 * b2, level),
    ]
    above, below = (place, level + 1), (place, level - 1)
    rows, width = conv_ref.shape
    r2, r4, r8 = rows // 2, rows // 4, rows // 8
    cut = width // 2
    halves = (slice(0, cut), slice(cut, width))
    bits = ((b1, b2), (b2, b1))
    across = ((mates[1], mates[2]), (mates[2], mates[1]))

    barrier = pltpu.get_barrier_semaphore()
    for mate in mates:
        pl.semaphore_signal(barrier, inc=1, device_id=mate, device_id_type=MESH)

    @pl.when(level < last)
    def _():
        pl.semaphore_signal(barrier, inc=1, device_id=above, device_id_type=MESH)

    @pl.when(level > 0)
    def _():
        pl.semaphore_signal(barrier, inc=1, device_id=below, device_id_type=MESH)

    pl.semaphore_wait(barrier, jnp.where((level == 0) | (level == last), 4, 5))

    def span(start, size):
        return pl.ds(pl.multiple_of(start, 16), size)

    mine = b0 * r2
    core_copy = remote(
        conv_ref.at[span((1 - b0) * r2, r2)], rx_core, core_send.at[0], core_recv.at[0], mates[0]
    )
    core_copy.start()

    def right(t, src):
        return remote(src, rx_line.at[t], right_send.at[t], right_recv.at[t], above)

    def left(t, src):
        slot = jnp.where(level - 1 == t, last + 1, t)
        return remote(src, rx_line.at[slot], left_send.at[t], left_recv.at[t], below)

    @pl.when(level == 0)
    def _():
        for t in range(last, 0, -1):
            right(t, part_ref.at[t]).start()

    @pl.when(level == last)
    def _():
        for t in range(last):
            left(t, part_ref.at[t]).start()

    def add_line(t):
        tx_line[t] = (part_ref[t].astype(f32) + rx_line[t].astype(f32)).astype(bf16)

    def pass_right(t, at):
        @pl.when(level == at)
        def _():
            right(t, part_ref.at[t]).wait_recv()
            add_line(t)
            right(t, tx_line.at[t]).start()

    def pass_left(t, at):
        @pl.when(level == at)
        def _():
            left(t, part_ref.at[t]).wait_recv()
            add_line(t)
            left(t, tx_line.at[t]).start()

    core_copy.wait_recv()
    total[...] = conv_ref[span(mine, r2), :].astype(f32) + rx_core[...].astype(f32)
    copies = []
    for h in range(2):
        first = bits[h][0]
        tx_two[h] = total[span((1 - first) * r4, r4), halves[h]].astype(bf16)
        copies.append(
            remote(tx_two.at[h], rx_two.at[h], two_send.at[h], two_recv.at[h], across[h][0])
        )
        copies[h].start()

    pass_right(3, 1)
    pass_left(0, 2)

    deeper = []
    for h in range(2):
        first, second = bits[h]
        copies[h].wait_recv()
        total[span(first * r4, r4), halves[h]] += rx_two[h].astype(f32)
        tx_three[h] = total[span(first * r4 + (1 - second) * r8, r8), halves[h]].astype(bf16)
        deeper.append(
            remote(
                tx_three.at[h], rx_three.at[h], three_send.at[h], three_recv.at[h], across[h][1]
            )
        )
        deeper[h].start()

    pass_right(3, 2)
    pass_left(0, 1)
    pass_right(2, 1)
    pass_left(1, 2)

    def back_copy(h, start, size, stage, mate):
        part = conv_out.at[span(start, size), halves[h]]
        return remote(part, part, back_send.at[stage, h], back_recv.at[stage, h], mate)

    stage_one, stage_two = [], []
    for h in range(2):
        first, second = bits[h]
        deeper[h].wait_recv()
        at = first * r4 + second * r8
        block = total[span(at, r8), halves[h]] + rx_three[h].astype(f32)
        conv_out[span(mine + at, r8), halves[h]] = block.astype(bf16)
        stage_one.append(back_copy(h, mine + at, r8, 0, across[h][1]))
        stage_one[h].start()
    for h in range(2):
        first = bits[h][0]
        stage_one[h].wait_recv()
        stage_two.append(back_copy(h, mine + first * r4, r4, 1, across[h][0]))
        stage_two[h].start()

    for t in range(last + 1):
        @pl.when(level == t)
        def _(t=t):
            block = part_ref[t].astype(f32)
            if t > 0:
                right(t, part_ref.at[t]).wait_recv()
                block = block + rx_line[t].astype(f32)
            if t < last:
                left(t, part_ref.at[t]).wait_recv()
                block = block + rx_line[last + 1].astype(f32)
            whole_out[own] = block.astype(bf16)

    def gather_copy(block, h, stage, mate):
        part = whole_out.at[block, :, halves[h]]
        k = 3 * h + stage
        return remote(part, part, gather_send.at[k], gather_recv.at[k], mate)

    one = own + 4 - 8 * b2, own + 2 - 4 * b1
    first_copies = [gather_copy(own, 0, 0, mates[2]), gather_copy(own, 1, 0, mates[1])]
    own_copies = [gather_copy(own, 0, 1, mates[1]), gather_copy(own, 1, 1, mates[2])]
    far_copies = [gather_copy(one[0], 0, 2, mates[1]), gather_copy(one[1], 1, 2, mates[2])]
    for h in range(2):
        first_copies[h].start()
        own_copies[h].start()

    for h in range(2):
        stage_two[h].wait_recv()
    region = conv_out.at[span(mine, r2)]
    core_back = remote(region, region, core_send.at[1], core_recv.at[1], mates[0])
    core_back.start()

    for h in range(2):
        first_copies[h].wait_recv()
        far_copies[h].start()

    def mate_copy(j, block):
        part = whole_out.at[block]
        return remote(part, part, gather_send.at[6 + j], gather_recv.at[6 + j], mates[0])

    blocks = [own, own + 2 - 4 * b1, own + 4 - 8 * b2, own + 6 - 4 * b1 - 8 * b2]
    mate_copies = [mate_copy(j, block) for j, block in enumerate(blocks)]
    mate_copies[0].start()
    for h in range(2):
        own_copies[h].wait_recv()
    mate_copies[1].start()
    mate_copies[2].start()
    for h in range(2):
        far_copies[h].wait_recv()
    mate_copies[3].start()

    core_copy.wait_send()
    core_back.wait()
    for j in range(4):
        mate_copies[j].wait()
    for h in range(2):
        copies[h].wait_send()
        deeper[h].wait_send()
        stage_one[h].wait_send()
        stage_two[h].wait_send()
        first_copies[h].wait_send()
        own_copies[h].wait_send()
        far_copies[h].wait_send()
    for t in range(last + 1):
        @pl.when(level < t)
        def _(t=t):
            right(t, part_ref.at[t]).wait_send()

        @pl.when(level > t)
        def _(t=t):
            left(t, part_ref.at[t]).wait_send()


def last_sums(conv, parts):
    rows, width = conv.shape
    levels, share, _ = parts.shape
    cut = width // 2
    dma = pltpu.SemaphoreType.DMA
    return pl.pallas_call(
        last_sums_kernel,
        in_specs=[whole_spec()] * 2,
        out_specs=[whole_spec()] * 2,
        out_shape=[
            jax.ShapeDtypeStruct((rows, width), bf16),
            jax.ShapeDtypeStruct((8, share, width), bf16),
        ],
        scratch_shapes=[
            pltpu.VMEM((rows // 2, width), f32),
            pltpu.VMEM((rows // 2, width), bf16),
            pltpu.VMEM((2, rows // 4, cut), bf16),
            pltpu.VMEM((2, rows // 4, cut), bf16),
            pltpu.VMEM((2, rows // 8, cut), bf16),
            pltpu.VMEM((2, rows // 8, cut), bf16),
            pltpu.VMEM((levels, share, width), bf16),
            pltpu.VMEM((levels + 1, share, width), bf16),
            dma((2,)),
            dma((2,)),
            dma((2,)),
            dma((2,)),
            dma((2,)),
            dma((2,)),
            dma((2, 2)),
            dma((2, 2)),
            dma((levels,)),
            dma((levels,)),
            dma((levels,)),
            dma((levels,)),
            dma((10,)),
            dma((10,)),
        ],
        compiler_params=pltpu.CompilerParams(
            collective_id=2, has_side_effects=True, vmem_limit_bytes=56 << 20
        ),
    )(conv, parts)


def on_device(
    block_input,
    row_order,
    conv_weight,
    batch_gain,
    batch_bias,
    first_gain,
    first_bias,
    w_query,
    w_key,
    w_value,
    relative_weight,
    content_bias,
    position_bias,
    w_out,
    second_gain,
    second_bias,
    w_inner,
    inner_bias,
    w_outer,
    cotangent,
):
    seq_count, length = row_order.shape
    group_rows = seq_count * length
    own_cols = block_input.shape[1]
    taps, _, width = conv_weight.shape
    reach = taps // 2
    pair, dk = content_bias.shape
    dv = w_value.shape[1] // pair
    qcols, vcols = pair * dk, pair * dv
    hidden_cols = w_inner.shape[1]
    features = relative_weight.shape[0]
    depth = lax.axis_size("mp")
    spread = lax.axis_size("dp")
    bits = spread.bit_length() - 1
    assert depth == 4 and seq_count == 2 and spread == 1 << bits and bits > 0
    place, level = lax.axis_index("dp"), lax.axis_index("mp")
    core = place % 2
    total_rows = group_rows * spread
    scale = dk ** (-0.5)
    half = length // 2


    def permute(value, route):
        pairs = []
        for d in range(spread):
            for z in range(depth):
                to = route(d, z)
                if to is not None:
                    pairs.append((d * depth + z, to[0] * depth + to[1]))
        return lax.ppermute(value, AXES, pairs)

    def swap_bit(value, bit):
        return permute(value, lambda d, z: (d ^ (1 << bit), z))

    def sum_dp(value):
        for bit in range(bits):
            value = value + swap_bit(value, bit)
        return value

    cell = min(8, spread)
    assert cell == 8
    cells = spread // cell
    inside = outside = None
    if cells > 1:
        inside = [[c * cell + i for i in range(cell)] for c in range(cells)]
        outside = [[c * cell + i for c in range(cells)] for i in range(cell)]

    def scatter_cell(value):
        value = lax.psum_scatter(value, "dp", scatter_dimension=0, axis_index_groups=inside)
        return value if cells == 1 else lax.psum(value, "dp", axis_index_groups=outside)

    order = jnp.where(core == 0, row_order, row_order[::-1])
    offsets = jnp.where(core == 0, jnp.array([0, length]), jnp.array([length, 0]))
    source = (order + offsets[:, None].astype(jnp.int32)).reshape(group_rows)
    rows = block_input[source].reshape(seq_count, length, own_cols)

    local = (w_inner.T, w_outer, w_out, jnp.concatenate([w_query.T, w_key.T, w_value.T], axis=0))
    local_rows = sum(value.shape[0] for value in local)
    share = lax.dynamic_slice_in_dim(
        jnp.concatenate(local, axis=0), place % cell * (local_rows // cell), local_rows // cell, 0
    )
    small = jnp.concatenate(
        [
            relative_weight.astype(f32),
            content_bias.reshape(1, qcols),
            position_bias.reshape(1, qcols),
            inner_bias.reshape(-1, qcols),
        ],
        axis=0,
    )
    conv_flat = conv_weight.reshape(taps * own_cols, width)
    resid_one, act_taps, stats, small, cot, weights = front(
        rows,
        batch_gain[None],
        batch_bias[None],
        conv_flat,
        share,
        small,
        cotangent.reshape(seq_count, 2, half, width),
        taps,
        bits,
        total_rows,
        min(256, half),
    )
    inner_weight = weights[:, :hidden_cols]
    outer_weight = weights[:, hidden_cols : 2 * hidden_cols]
    out_weight = weights[:, 2 * hidden_cols : 2 * hidden_cols + vcols]
    qkv_weight = weights[:, 2 * hidden_cols + vcols :]
    batch_mean, batch_scale = stats[0], stats[1]

    rel_weight = small[:, :features].astype(bf16)
    content_all = small[:, features][:, None, :]
    position_all = small[:, features + 1][:, None, :]
    inner_bias_all = small[:, features + 2 :].reshape(depth, 1, hidden_cols)
    basis = relative_basis(length, features)
    basis = jnp.where(jnp.arange(2 * length)[:, None] < 2 * length - 1, basis, 0.0).astype(bf16)
    basis = lax.dynamic_slice_in_dim(basis, half * (1 - core), length + half, 0)
    rel_keys = jnp.einsum(
        "wf,zfq->zwq", basis, rel_weight, preferred_element_type=f32
    ).astype(bf16)

    normed_one, unit_one, inverse_one = norm_rows(resid_one, first_gain, first_bias)
    normed_one = normed_one.astype(bf16)
    qkv = jnp.einsum("rd,znd->zrn", normed_one, qkv_weight, preferred_element_type=f32)
    query = qkv[:, :, :qcols] * scale
    query_w = (query + content_all).astype(bf16)
    query_r = (query + position_all).astype(bf16)
    kv_own = qkv[:, :, qcols:].astype(bf16)
    kv_other = swap_bit(kv_own, 0)
    kv = jnp.concatenate(
        [jnp.where(core == 0, kv_own, kv_other), jnp.where(core == 0, kv_other, kv_own)], axis=1
    )
    bq = min(256, half)
    attended, prob = attend(query_w, query_r, kv, rel_keys, dk, dv, bq)
    resid_two = resid_one + jnp.einsum(
        "zrn,znd->rd", attended, out_weight, preferred_element_type=f32
    )
    normed_two, unit_two, inverse_two = norm_rows(resid_two, second_gain, second_bias)
    normed_two = normed_two.astype(bf16)
    inner = (
        jnp.einsum("rd,znd->zrn", normed_two, inner_weight, preferred_element_type=f32)
        + inner_bias_all
    )
    hidden = gelu(inner).astype(bf16)
    block_output = (
        resid_two + jnp.einsum("zrn,znd->rd", hidden, outer_weight, preferred_element_type=f32)
    ).astype(bf16)
    block_output = permute(
        block_output, lambda d, z: (d - d % 2 + z // 2, 2 * (z % 2) + d % 2)
    )

    d_hidden = jnp.einsum("rd,znd->zrn", cot, outer_weight, preferred_element_type=f32)
    d_inner32 = d_hidden * gelu_slope(inner)
    d_inner = d_inner32.astype(bf16)
    g_inner_bias = jnp.sum(d_inner.astype(f32), axis=1)
    d_norm_two = jnp.einsum("zrn,znd->rd", d_inner, inner_weight, preferred_element_type=f32)
    feed_grads = weight_grads([(hidden, cot), (d_inner, normed_two)], None, cell)
    feed_parts = scatter_cell(feed_grads)
    g_second_gain = jnp.sum(d_norm_two * unit_two, axis=0)
    g_second_bias = jnp.sum(d_norm_two, axis=0)
    d_resid_two = cot.astype(f32) + norm_back(d_norm_two, unit_two, inverse_two, second_gain)

    d_two, _ = lax.optimization_barrier((d_resid_two.astype(bf16), feed_grads))
    d_attended = jnp.einsum("rd,znd->zrn", d_two, out_weight, preferred_element_type=f32)
    d_attended = d_attended.astype(bf16)
    d_query, query_sums, d_kv, d_rel = attend_back(
        query_w, query_r, kv, rel_keys, prob, d_attended, dk, dv, bq, scale
    )
    d_kv_give = lax.dynamic_slice_in_dim(d_kv, (1 - core) * half, half, 1)
    d_kv_keep = lax.dynamic_slice_in_dim(d_kv, core * half, half, 1)
    d_kv_own = (d_kv_keep.astype(f32) + swap_bit(d_kv_give, 0).astype(f32)).astype(bf16)
    d_qkv = jnp.concatenate([d_query, d_kv_own], axis=2)
    d_norm_one = jnp.einsum("zrn,znd->rd", d_qkv, qkv_weight, preferred_element_type=f32)
    g_first_gain = jnp.sum(d_norm_one * unit_one, axis=0)
    g_first_bias = jnp.sum(d_norm_one, axis=0)
    d_resid_one = (
        d_resid_two + norm_back(d_norm_one, unit_one, inverse_one, first_gain)
    ).astype(bf16)

    g_relative = jnp.einsum("wf,zwq->zfq", basis, d_rel, preferred_element_type=f32)
    of_level = jnp.concatenate(
        [
            g_relative.reshape(depth, -1),
            query_sums[:, 0],
            query_sums[:, 1],
            g_inner_bias,
        ],
        axis=1,
    )
    of_all = jnp.concatenate([g_first_gain, g_first_bias, g_second_gain, g_second_bias])
    of_all = jnp.broadcast_to(of_all[None], (depth, 4 * width))
    extra = jnp.concatenate([of_all, of_level], axis=1)
    used = extra.shape[1]
    extra_rows = -(-used // (cell * width))
    extra = jnp.pad(extra, ((0, 0), (0, extra_rows * cell * width - used)))
    extra = jnp.swapaxes(extra.reshape(depth, cell, extra_rows, width), 0, 1)
    extra = jnp.pad(extra, ((0, 0), (0, 0), (0, -extra_rows % 16), (0, 0))).astype(bf16)
    attend_grads = weight_grads([(attended, d_two), (d_qkv, normed_one)], extra, cell)

    d_act, d_cols, g_conv, attend_parts, _ = conv_back(
        d_resid_one, act_taps, conv_flat, attend_grads, taps, min(256, half)
    )
    d_act = d_act.reshape(group_rows, own_cols)
    centred = (rows.reshape(group_rows, own_cols).astype(f32) - batch_mean) * batch_scale
    pre_act = batch_gain * centred + batch_bias
    d_pre = d_act * gelu_slope(pre_act)
    batch_sums = sum_dp(jnp.stack([jnp.sum(d_pre * centred, axis=0), jnp.sum(d_pre, axis=0)]))
    g_batch_gain, g_batch_bias = batch_sums[0], batch_sums[1]
    d_shifted = d_cols.reshape(group_rows, own_cols).astype(f32)
    d_shifted = d_shifted + batch_gain * batch_scale * (
        d_pre - g_batch_bias / total_rows - centred * g_batch_gain / total_rows
    )
    grad_input = jnp.zeros((group_rows, own_cols), f32).at[source].set(d_shifted)

    if cells > 1:
        attend_parts = lax.psum(attend_parts, "dp", axis_index_groups=outside)
        g_conv = lax.psum(g_conv, "dp", axis_index_groups=outside)
    parts = jnp.concatenate([feed_parts, attend_parts], axis=1)
    g_conv, whole = last_sums(g_conv, parts)
    g_conv = g_conv.astype(f32).reshape(taps, own_cols, width)
    whole = whole.astype(f32)
    sums, at = [], 0
    for cols in (hidden_cols, hidden_cols, vcols, 2 * qcols + vcols):
        sums.append(whole[:, at : at + cols // cell].reshape(cols, width))
        at += cols // cell
    g_outer, g_inner, g_out, g_qkv = sums
    rest = whole[:, at : at + extra_rows].reshape(-1)[:used]

    def take(start, size):
        return rest[start : start + size]

    base = 4 * width
    rel_size = features * qcols

    return (
        block_output,
        grad_input,
        g_conv,
        g_batch_gain,
        g_batch_bias,
        take(0, width),
        take(width, width),
        g_qkv[:qcols].T,
        g_qkv[qcols : 2 * qcols].T,
        g_qkv[2 * qcols :].T,
        take(base, rel_size).reshape(features, qcols),
        take(base + rel_size, qcols).reshape(pair, dk),
        take(base + rel_size + qcols, qcols).reshape(pair, dk),
        g_out,
        take(2 * width, width),
        take(3 * width, width),
        g_inner.T,
        take(base + rel_size + 2 * qcols, hidden_cols),
        g_outer,
    )


def solution(mesh):
    return jax.shard_map(
        on_device,
        mesh=mesh,
        in_specs=(
            P("dp", "mp"),
            P("dp", None),
            P(None, "mp", None),
            P("mp"),
            P("mp"),
            P(),
            P(),
            P(None, "mp"),
            P(None, "mp"),
            P(None, "mp"),
            P(None, "mp"),
            P("mp", None),
            P("mp", None),
            P("mp", None),
            P(),
            P(),
            P(None, "mp"),
            P("mp"),
            P("mp", None),
            P("dp", None),
        ),
        out_specs=(
            P(("dp", "mp"), None),
            P("dp", "mp"),
            P(None, "mp", None),
            P("mp"),
            P("mp"),
            P(),
            P(),
            P(None, "mp"),
            P(None, "mp"),
            P(None, "mp"),
            P(None, "mp"),
            P("mp", None),
            P("mp", None),
            P("mp", None),
            P(),
            P(),
            P(None, "mp"),
            P("mp"),
            P("mp", None),
        ),
        check_vma=False,
    )
```

```python
import functools
import math

import jax
import jax.numpy as jnp
from jax import lax
from jax.experimental import pallas as pl
from jax.experimental.pallas import tpu as pltpu
from jax.sharding import PartitionSpec as P

EPSILON = 1e-05
f32 = jnp.float32
bf16 = jnp.bfloat16
AXES = ("dp", "mp")
MESH = pl.DeviceIdType.MESH
NT = (((1,), (1,)), ((), ()))
TN = (((0,), (0,)), ((), ()))
NN = (((1,), (0,)), ((), ()))


def dot(a, b, dims=NN):
    return lax.dot_general(a, b, dims, preferred_element_type=f32)


def gelu(value):
    return value * jax.nn.sigmoid(1.702 * value)


def gelu_slope(value):
    sig = jax.nn.sigmoid(1.702 * value)
    return sig + 1.702 * value * sig * (1.0 - sig)


def norm_rows(rows, gain, bias):
    centre = rows - jnp.mean(rows, axis=-1, keepdims=True)
    spread = jnp.mean(centre * centre, axis=-1, keepdims=True)
    inverse = lax.rsqrt(spread + EPSILON)
    unit = centre * inverse
    return (unit * gain + bias, unit, inverse)


def norm_back(grad, unit, inverse, gain):
    scaled = grad * gain
    return inverse * (
        scaled
        - jnp.mean(scaled, axis=-1, keepdims=True)
        - unit * jnp.mean(scaled * unit, axis=-1, keepdims=True)
    )


def relative_basis(length, features):
    distance = jnp.arange(2 * length, dtype=f32) - (length - 1)
    half = features // 2
    ratio = jnp.arange(half, dtype=f32) / (half - 1)
    life = jnp.power(jnp.float32(length), ratio)
    decay = jnp.exp(-math.log(2.0) * jnp.abs(distance)[:, None] / life[None, :])
    return jnp.concatenate([decay, jnp.sign(distance)[:, None] * decay], axis=1)


def attend_kernel(dk, dv, bq, qw_ref, qr_ref, kv_ref, rel_ref, out_ref, prob_ref):
    rows, length = qw_ref.shape[1], kv_ref.shape[1]
    width = length + bq
    pair = qw_ref.shape[2] // dk
    lane = lax.broadcasted_iota(jnp.int32, (bq, pair * dk), 1) // dk
    keys = kv_ref[0, :, : pair * dk]
    for b in range(rows // bq):
        at = slice(b * bq, (b + 1) * bq)
        lo = rows - (b + 1) * bq
        window = rel_ref[0, lo : lo + width, :]
        qw, qr = qw_ref[0, at, :], qr_ref[0, at, :]
        zero = jnp.zeros_like(qw)
        mixed = []
        for h in range(pair):
            content = dot(jnp.where(lane == h, qw, zero), keys, NT)
            place = dot(jnp.where(lane == h, qr, zero), window, NT)
            place = pltpu.roll(place, width - (bq - 1), 1, stride=1, stride_axis=0)
            logits = content + place[:, :length]
            weights = jnp.exp(logits - jnp.max(logits, axis=1, keepdims=True))
            prob = (weights * (1.0 / jnp.sum(weights, axis=1, keepdims=True))).astype(bf16)
            prob_ref[0, h, at, :] = prob
            values = kv_ref[0, :, pair * dk + h * dv : pair * dk + (h + 1) * dv]
            mixed.append(dot(prob, values).astype(bf16))
        out_ref[0, at, :] = jnp.concatenate(mixed, axis=1)


def block_spec(*shape):
    return pl.BlockSpec((1,) + shape, lambda g: (g,) + (0,) * len(shape))


def attend(qw, qr, kv, rel, dk, dv, bq):
    groups, rows, qcols = qw.shape
    length, kvcols = kv.shape[1:]
    pair = qcols // dk
    return pl.pallas_call(
        functools.partial(attend_kernel, dk, dv, bq),
        grid=(groups,),
        in_specs=[
            block_spec(rows, qcols),
            block_spec(rows, qcols),
            block_spec(length, kvcols),
            block_spec(rel.shape[1], qcols),
        ],
        out_specs=[block_spec(rows, pair * dv), block_spec(pair, rows, length)],
        out_shape=[
            jax.ShapeDtypeStruct((groups, rows, pair * dv), bf16),
            jax.ShapeDtypeStruct((groups, pair, rows, length), bf16),
        ],
        compiler_params=pltpu.CompilerParams(vmem_limit_bytes=50 << 20),
    )(qw, qr, kv, rel)


def attend_back_kernel(
    dk, dv, bq, scale, qw_ref, qr_ref, kv_ref, rel_ref, prob_ref, dmix_ref,
    dq_ref, sums_ref, dkv_ref, drel_ref, dkt, dvt, drt,
):
    rows, length = qw_ref.shape[1], kv_ref.shape[1]
    width = length + bq
    pair = qw_ref.shape[2] // dk
    qcols = pair * dk
    lane = lax.broadcasted_iota(jnp.int32, (bq, qcols), 1) // dk
    across = lax.broadcasted_iota(jnp.int32, (bq, bq), 0)
    across = across + lax.broadcasted_iota(jnp.int32, (bq, bq), 1)
    flip = jnp.where(across == bq - 1, 1.0, 0.0).astype(bf16)
    keys = kv_ref[0, :, :qcols]
    sums_w = jnp.zeros((1, qcols), f32)
    sums_r = jnp.zeros((1, qcols), f32)
    drt[...] = jnp.zeros_like(drt)
    for b in range(rows // bq):
        at = slice(b * bq, (b + 1) * bq)
        lo = rows - (b + 1) * bq
        window = rel_ref[0, lo : lo + width, :]
        qw, qr = qw_ref[0, at, :], qr_ref[0, at, :]
        zero = jnp.zeros_like(qw)
        qr_flip = dot(flip, qr).astype(bf16)
        dqw = jnp.zeros((bq, qcols), f32)
        dqr = jnp.zeros((bq, qcols), f32)
        for h in range(pair):
            prob = prob_ref[0, h, at, :]
            values = kv_ref[0, :, qcols + h * dv : qcols + (h + 1) * dv]
            dmix = dmix_ref[0, at, h * dv : (h + 1) * dv]
            prob32 = prob.astype(f32)
            part = dot(dmix, values, NT) * prob32
            d_logits = part - prob32 * jnp.sum(part, axis=1, keepdims=True)
            d_logits = d_logits.astype(bf16)
            turned = jnp.concatenate(
                [dot(flip, d_logits), jnp.zeros((bq, width - length), f32)], axis=1
            )
            d_window = pltpu.roll(turned, 0, 1, stride=1, stride_axis=0).astype(bf16)
            dqw = dqw + jnp.where(lane == h, dot(d_logits, keys), 0.0)
            dqr = dqr + jnp.where(lane == h, dot(d_window, window), 0.0)
            key_part = dot(jnp.where(lane == h, qw, zero), d_logits, TN)
            value_part = dot(dmix, prob, TN)
            if b == 0 and h == 0:
                dkt[...] = key_part
            else:
                dkt[...] += key_part
            if b == 0:
                dvt[h] = value_part
            else:
                dvt[h] += value_part
            drt[:, lo : lo + width] += dot(jnp.where(lane == h, qr_flip, zero), d_window, TN)
        high = dqr.astype(bf16)
        dqr = dot(flip, high) + dot(flip, (dqr - high.astype(f32)).astype(bf16))
        sums_w += jnp.sum(dqw, axis=0, keepdims=True)
        sums_r += jnp.sum(dqr, axis=0, keepdims=True)
        dq_ref[0, at, :] = ((dqw + dqr) * scale).astype(bf16)
    sums_ref[0] = jnp.concatenate([sums_w, sums_r, jnp.zeros((6, qcols), f32)], axis=0)
    dkv_ref[0, :, :qcols] = dkt[...].T.astype(bf16)
    for h in range(pair):
        dkv_ref[0, :, qcols + h * dv : qcols + (h + 1) * dv] = dvt[h].T.astype(bf16)
    drel_ref[0] = drt[...].T.astype(bf16)


def attend_back(qw, qr, kv, rel, prob, dmix, dk, dv, bq, scale):
    groups, rows, qcols = qw.shape
    length, kvcols = kv.shape[1:]
    pair = qcols // dk
    rels = rel.shape[1]
    return pl.pallas_call(
        functools.partial(attend_back_kernel, dk, dv, bq, scale),
        grid=(groups,),
        in_specs=[
            block_spec(rows, qcols),
            block_spec(rows, qcols),
            block_spec(length, kvcols),
            block_spec(rels, qcols),
            block_spec(pair, rows, length),
            block_spec(rows, pair * dv),
        ],
        out_specs=[
            block_spec(rows, qcols),
            block_spec(8, qcols),
            block_spec(length, kvcols),
            block_spec(rels, qcols),
        ],
        out_shape=[
            jax.ShapeDtypeStruct((groups, rows, qcols), bf16),
            jax.ShapeDtypeStruct((groups, 8, qcols), f32),
            jax.ShapeDtypeStruct((groups, length, kvcols), bf16),
            jax.ShapeDtypeStruct((groups, rels, qcols), bf16),
        ],
        scratch_shapes=[
            pltpu.VMEM((qcols, length), f32),
            pltpu.VMEM((pair, dv, length), f32),
            pltpu.VMEM((qcols, rels), f32),
        ],
        compiler_params=pltpu.CompilerParams(vmem_limit_bytes=50 << 20),
    )(qw, qr, kv, rel, prob, dmix)


def line_of():
    core, level = lax.axis_index("dp") % 2, lax.axis_index("mp")
    depth = lax.axis_size("mp")
    rank = jnp.where(core == 0, level, depth - 1 - level)
    step = jnp.where(core == 0, 1, -1)
    place = lax.axis_index("dp")
    up, down, sibling = (place, level + step), (place, level - step), (place + 1 - 2 * core, level)
    return core, level, rank, up, down, sibling


def remote(src, dst, send_sem, recv_sem, device):
    return pltpu.make_async_remote_copy(
        src_ref=src,
        dst_ref=dst,
        send_sem=send_sem,
        recv_sem=recv_sem,
        device_id=device,
        device_id_type=MESH,
    )


def greet(rank, last, up, down, mates):
    barrier = pltpu.get_barrier_semaphore()

    @pl.when(rank < last)
    def _():
        pl.semaphore_signal(barrier, inc=1, device_id=up, device_id_type=MESH)

    @pl.when(rank > 0)
    def _():
        pl.semaphore_signal(barrier, inc=1, device_id=down, device_id_type=MESH)

    for mate in mates:
        pl.semaphore_signal(barrier, inc=1, device_id=mate, device_id_type=MESH)
    ends = (rank == 0) | (rank == last)
    pl.semaphore_wait(barrier, jnp.where(ends, 1 + len(mates), 2 + len(mates)))


def mate_of(place, level, bit):
    return place + (1 << bit) - (2 << bit) * (place // (1 << bit) % 2), level


class Both:
    def __init__(self, *copies):
        self.copies = copies

    def start(self):
        for copy in self.copies:
            copy.start()

    def wait_recv(self):
        for copy in self.copies:
            copy.wait_recv()

    def wait_send(self):
        for copy in self.copies:
            copy.wait_send()


def diagonal(size):
    row = lax.broadcasted_iota(jnp.int32, (1, size, size), 1)
    return jnp.where(row == lax.broadcasted_iota(jnp.int32, (1, size, size), 2), 1.0, 0.0)


def encode(rows, whole_ref, step_ref):
    step = jnp.max(jnp.abs(rows), axis=1, keepdims=True) * (1.0 / 32000.0)
    scaled = jnp.round(rows * (1.0 / jnp.maximum(step, 1e-30)))
    whole_ref[...] = scaled.astype(jnp.int32).astype(jnp.int16)
    step = step.reshape(rows.shape[0] // 128, 128, 1)
    step_ref[: step.shape[0], :] = jnp.sum(step * diagonal(128), axis=1)


def decode(whole_ref, step_ref):
    count = whole_ref.shape[0]
    step = step_ref[: count // 128, :].reshape(count // 128, 1, 128)
    step = jnp.sum(step * diagonal(128), axis=2, keepdims=True).reshape(count, 1)
    return whole_ref[...].astype(jnp.int32).astype(f32) * step


def front_kernel(
    chunk, taps, bits, total_rows,
    rows_ref, affine_ref, w_ref, share_ref, small_ref, cot_ref,
    resid_ref, act_ref, stats_ref, small_out, cot_out, weights_ref,
    acc, rx_far, rx_near, rx_back, tx_far, tx_near, stage, rx_half, tx_stats, rx_stats,
    rx_far_step, rx_near_step, rx_back_step, tx_far_step, tx_near_step,
    far_send, far_recv, near_send, near_recv, back_recv, swap_send, swap_recv,
    step_send, step_recv,
    stats_send, stats_recv, small_send, small_recv, cot_send, cot_recv, own_sem,
    up_send, down_send, level_recv, plane_send, plane_recv, cross_send, cross_recv,
    core_send, core_recv,
):
    core, level, rank, up, down, sibling = line_of()
    place = lax.axis_index("dp")
    levels = lax.axis_size("mp")
    own = place % 8
    seqs, length, own_cols = rows_ref.shape
    width = w_ref.shape[1]
    half = length // 2
    reach = taps // 2
    count = length // chunk
    per_half = count // 2
    assert count == 4
    tile = min(512, width)
    cut = width // 2
    mates = [mate_of(place, level, bit) for bit in range(bits)]

    barrier = pltpu.get_barrier_semaphore()
    for r in range(1, 4):
        other = (place, (level + r) % levels)
        pl.semaphore_signal(barrier, inc=1, device_id=other, device_id_type=MESH)
    for mate in mates:
        pl.semaphore_signal(barrier, inc=1, device_id=mate, device_id_type=MESH)

    values = rows_ref[...].astype(f32).reshape(seqs * length, own_cols)
    sums = jnp.sum(values, axis=0, keepdims=True)
    squares = jnp.sum(values * values, axis=0, keepdims=True)
    sums = jnp.concatenate([sums, squares, jnp.zeros((6, own_cols), f32)], axis=0)
    pl.semaphore_wait(barrier, 3 + bits)

    x_mate, y_mate = mates[1], mates[2]
    cross = [own + 2 - 4 * (own // 2 % 2), own + 4 - 8 * (own // 4)]
    corner = cross[0] + cross[1] - own
    left_half, right_half = slice(0, cut), slice(cut, width)

    def piece_at(q):
        base = jnp.where((level == 0) | (level == 3), q, jnp.where(q == 0, 1, jnp.where(q == 1, 0, q)))
        return jnp.where(level < 2, base, 3 - base)

    share_rows = share_ref.shape[0]

    def piece(z, block):
        return weights_ref.at[z, pl.ds(pl.multiple_of(block * share_rows, 16), share_rows)]

    def send(part, sems, device):
        return remote(part, part, sems[0], sems[1], device)

    def up_copy(z):
        return send(piece(z, own), (up_send.at[z], level_recv.at[z]), (place, level + 1))

    def down_copy(z):
        return send(piece(z, own), (down_send.at[z], level_recv.at[z]), (place, level - 1))

    def plane_copy(z, k):
        sems = (plane_send.at[z, k], plane_recv.at[z, k])
        return send(piece(z, own), sems, (x_mate, y_mate)[k])

    def cross_copy(z, k):
        part = piece(z, cross[1 - k]).at[:, (left_half, right_half)[k]]
        return send(part, (cross_send.at[z, k], cross_recv.at[z, k]), (x_mate, y_mate)[k])

    def core_copy(z, k):
        part = piece(z, (own, cross[0], cross[1], corner)[k])
        return send(part, (core_send.at[z, k], core_recv.at[z, k]), sibling)

    def weights_first(q):
        z = piece_at(q)

        @pl.when(z != level)
        def _():
            up_copy(z).wait_recv()

        @pl.when((z <= level) & (level < 3))
        def _():
            up_copy(z).start()

        @pl.when((z >= level) & (level > 0))
        def _():
            down_copy(z).start()

        plane_copy(z, 0).start()
        plane_copy(z, 1).start()
        core_copy(z, 0).start()

    def weights_second(q):
        z = piece_at(q)
        plane_copy(z, 0).wait_recv()
        plane_copy(z, 1).wait_recv()
        cross_copy(z, 0).start()
        cross_copy(z, 1).start()
        core_copy(z, 1).start()
        core_copy(z, 2).start()

    def weights_third(q):
        z = piece_at(q)
        cross_copy(z, 0).wait_recv()
        cross_copy(z, 1).wait_recv()
        core_copy(z, 3).start()

    def weights_fourth(q):
        z = piece_at(q)
        for k in range(4):
            core_copy(z, k).wait_recv()

    stages = (weights_first, weights_second, weights_third, weights_fourth)
    plans = (
        (rank == 0, ((-1, 4, 4, 6), (4, 6, 7, 8), (5, 7, 8, 8), (8, 8, 8, 8))),
        ((rank == 1) | (rank == 2), ((-1, 0, 0, 2), (1, 3, 4, 6), (3, 5, 6, 8), (5, 7, 8, 8))),
        (rank == 3, ((-1, 3, 5, 7), (2, 6, 8, 8), (4, 7, 8, 8), (8, 8, 8, 8))),
    )

    def weights_turn(i):
        for mine, plan in plans:
            for stage, turns in zip(stages, plan):
                for q, turn in enumerate(turns):
                    if isinstance(i, int):
                        if turn == i:
                            pl.when(mine)(functools.partial(stage, q))
                    elif 0 <= turn < 2 * count:
                        pl.when(mine & (i == turn))(functools.partial(stage, q))

    own_copy = pltpu.make_async_copy(share_ref, piece(level, own), own_sem)
    own_copy.start()

    def small_copy(r):
        other = (place, (level + r) % levels)
        sems = (small_send.at[r - 1], small_recv.at[level])
        return remote(small_ref, small_out.at[level], sems[0], sems[1], other)

    for r in range(1, 4):
        small_copy(r).start()
    small_out[level] = small_ref[...]
    cot_copy = remote(cot_ref.at[level % 2, 1 - core], cot_out, cot_send, cot_recv, sibling)
    cot_keep = pltpu.make_async_copy(cot_ref.at[level % 2, core], cot_out, cot_recv)

    @pl.when(rank < 2)
    def _():
        cot_copy.start()
        cot_keep.start()

    own_copy.wait()

    for bit in range(bits):
        tx_stats[bit] = sums
        copy = remote(
            tx_stats.at[bit], rx_stats.at[bit], stats_send.at[bit], stats_recv.at[bit], mates[bit]
        )
        copy.start()
        copy.wait()
        sums = sums + rx_stats[bit]
    weights_first(0)
    mean = sums[0:1] / total_rows
    scale = lax.rsqrt(sums[1:2] / total_rows - mean * mean + EPSILON)
    stats_ref[...] = jnp.concatenate([mean, scale, jnp.zeros((6, own_cols), f32)], axis=0)
    row = lax.broadcasted_iota(jnp.int32, (length, own_cols), 0)
    for seq in range(seqs):
        centred = (rows_ref[seq].astype(f32) - mean) * scale
        act = gelu(affine_ref[0:1, :] * centred + affine_ref[1:2, :])
        for t in range(taps):
            moved = pltpu.roll(act, (reach - t) % length, 0) if t != reach else act
            inside = (row + (t - reach) >= 0) & (row + (t - reach) < length)
            act_ref[seq, :, t * own_cols : (t + 1) * own_cols] = jnp.where(
                inside, moved, 0.0
            ).astype(bf16)

    def line_copy(c, whole, step, sems, k, device):
        rows = pl.ds(pl.multiple_of(c * chunk, chunk), chunk)
        return Both(
            remote(whole[0].at[rows], whole[1].at[rows], sems[0].at[c], sems[1].at[c], device),
            remote(
                step[0].at[c], step[1].at[c], step_send.at[min(k, 1), c], step_recv.at[k, c], device
            ),
        )

    def far_copy(c):
        step = (tx_far_step, rx_far_step)
        return line_copy(c, (tx_far, rx_far), step, (far_send, far_recv), 0, down)

    def near_copy(c):
        step = (tx_near_step, rx_near_step)
        return line_copy(c, (tx_near, rx_near), step, (near_send, near_recv), 1, down)

    def back_copy(c):
        step = (tx_near_step, rx_back_step)
        return line_copy(c, (tx_near, rx_back), step, (near_send, back_recv), 2, up)

    def swap_copy(h):
        rows = pl.ds(h * chunk, chunk)
        return remote(stage.at[rows], rx_half.at[rows], swap_send.at[h], swap_recv.at[h], sibling)

    def finish(c):
        rows = pl.ds(c % per_half * chunk, chunk)

        @pl.when(c // per_half == core)
        def _():
            resid_ref[rows, :] = acc[...]

        @pl.when(c // per_half != core)
        def _():
            stage[rows, :] = acc[...]
            swap_copy(c % per_half).start()

    def step(i, _):
        weights_turn(i)
        c = i % count
        near = jnp.where(rank == 0, i < count, i >= count)
        seq = jnp.where(near, 1, 0)
        rows = pl.ds(pl.multiple_of(c * chunk, chunk), chunk)
        for n in range(width // tile):
            cols = slice(n * tile, (n + 1) * tile)
            acc[:, cols] = dot(act_ref[seq, rows, :], w_ref[:, cols])
        here = pl.ds(pl.multiple_of(level * own_cols, 128), own_cols)
        acc[:, here] += rows_ref[seq, rows, :].astype(f32)

        @pl.when(jnp.logical_not(near))
        def _():
            @pl.when(rank < 3)
            def _():
                far_copy(c).wait_recv()
                acc[...] += decode(rx_far.at[rows], rx_far_step.at[c])

            @pl.when(rank > 0)
            def _():
                encode(acc[...], tx_far.at[rows], tx_far_step.at[c])

                @pl.when(c >= 2)
                def _():
                    far_copy(c - 2).wait_send()

                far_copy(c).start()

            @pl.when(rank == 0)
            def _():
                finish(c)

                @pl.when(c >= 1)
                def _():
                    back_copy(c - 1).wait_send()

                back_copy(c).start()

        @pl.when(near)
        def _():
            @pl.when((rank == 1) | (rank == 2))
            def _():
                near_copy(c).wait_recv()
                acc[...] += decode(rx_near.at[rows], rx_near_step.at[c])

            @pl.when(rank == 1)
            def _():
                back_copy(c).wait_recv()
                acc[...] += decode(rx_back.at[rows], rx_back_step.at[c])
                finish(c)

            @pl.when(rank != 1)
            def _():
                encode(acc[...], tx_near.at[rows], tx_near_step.at[c])

            @pl.when(rank >= 2)
            def _():
                @pl.when(c < 2)
                def _():
                    far_copy(count - 2 + c).wait_send()

                @pl.when(c >= 2)
                def _():
                    near_copy(c - 2).wait_send()

                near_copy(c).start()

        return 0

    lax.fori_loop(0, 2 * count, step, 0)
    weights_turn(2 * count)

    @pl.when(rank >= 2)
    def _():
        def take(h, _):
            rows = pl.ds(pl.multiple_of(h * chunk, chunk), chunk)
            swap_copy(h).wait_recv()
            resid_ref[rows, :] = rx_half[rows, :]
            return 0

        lax.fori_loop(0, per_half, take, 0)
        cot_copy.wait_recv()

    @pl.when(rank < 2)
    def _():
        lax.fori_loop(0, per_half, lambda h, _: (swap_copy(h).wait_send(), 0)[1], 0)
        cot_copy.wait_send()
        cot_keep.wait()

    @pl.when(rank == 1)
    def _():
        far_copy(count - 2).wait_send()
        far_copy(count - 1).wait_send()

    @pl.when(rank >= 2)
    def _():
        near_copy(count - 2).wait_send()
        near_copy(count - 1).wait_send()

    @pl.when(rank == 0)
    def _():
        back_copy(count - 1).wait_send()

    for r in range(1, 4):
        small_copy(r).wait_send()
        other = (level + r) % levels
        part = small_out.at[other]
        remote(part, part, small_send.at[r - 1], small_recv.at[other], sibling).wait_recv()

    def end(z, _):
        @pl.when((z <= level) & (level < 3))
        def _():
            up_copy(z).wait_send()

        @pl.when((z >= level) & (level > 0))
        def _():
            down_copy(z).wait_send()

        for k in range(2):
            plane_copy(z, k).wait_send()
            cross_copy(z, k).wait_send()
        for k in range(4):
            core_copy(z, k).wait_send()
        return 0

    lax.fori_loop(0, levels, end, 0)


def whole_spec():
    return pl.BlockSpec(memory_space=pltpu.VMEM)


def any_spec():
    return pl.BlockSpec(memory_space=pl.ANY)


def front(rows, affine, weight, share, small, cot, taps, bits, total_rows, chunk):
    seqs, length, own_cols = rows.shape
    depth, width = weight.shape
    levels = lax.axis_size("mp")
    half, count = length // 2, length // chunk
    dma = pltpu.SemaphoreType.DMA
    shape = jax.ShapeDtypeStruct
    return pl.pallas_call(
        functools.partial(front_kernel, chunk, taps, bits, total_rows),
        in_specs=[whole_spec()] * 5 + [any_spec()],
        out_specs=[whole_spec()] * 5 + [any_spec()],
        out_shape=[
            shape((half, width), f32),
            shape((seqs, length, depth), bf16),
            shape((8, own_cols), f32),
            shape((levels,) + small.shape, f32),
            shape((half, width), bf16),
            shape((levels, 8 * share.shape[0], width), bf16),
        ],
        scratch_shapes=[
            pltpu.VMEM((chunk, width), f32),
            pltpu.VMEM((length, width), jnp.int16),
            pltpu.VMEM((length, width), jnp.int16),
            pltpu.VMEM((length, width), jnp.int16),
            pltpu.VMEM((length, width), jnp.int16),
            pltpu.VMEM((length, width), jnp.int16),
            pltpu.VMEM((half, width), f32),
            pltpu.VMEM((half, width), f32),
            pltpu.VMEM((bits, 8, own_cols), f32),
            pltpu.VMEM((bits, 8, own_cols), f32),
            pltpu.VMEM((count, 8, 128), f32),
            pltpu.VMEM((count, 8, 128), f32),
            pltpu.VMEM((count, 8, 128), f32),
            pltpu.VMEM((count, 8, 128), f32),
            pltpu.VMEM((count, 8, 128), f32),
            dma((count,)),
            dma((count,)),
            dma((count,)),
            dma((count,)),
            dma((count,)),
            dma((count // 2,)),
            dma((count // 2,)),
            dma((2, count)),
            dma((3, count)),
            dma((bits,)),
            dma((bits,)),
            dma((3,)),
            dma((levels,)),
            dma(()),
            dma(()),
            dma(()),
            dma((levels,)),
            dma((levels,)),
            dma((levels,)),
            dma((levels, 2)),
            dma((levels, 2)),
            dma((levels, 2)),
            dma((levels, 2)),
            dma((levels, 4)),
            dma((levels, 4)),
        ],
        cost_estimate=pl.CostEstimate(
            flops=4 * length * depth * width, bytes_accessed=400 << 20, transcendentals=0
        ),
        compiler_params=pltpu.CompilerParams(
            collective_id=0, has_side_effects=True, vmem_limit_bytes=56 << 20
        ),
    )(rows, affine, weight, share, small, cot)


def conv_back_kernel(
    chunk, taps, grad_ref, act_ref, w_ref, other_ref, dact_ref, dcol_ref, gw_ref, part_ref, rx_one,
    whole, gsum, acc, own_sum, loaded, rx_two, rx_three,
    half_send, half_recv, far_send, far_recv, near_send, near_recv, back_send, back_recv,
    keep_sem, out_sem, own_sem, load_sem, one_send, one_recv, two_send, two_recv, three_send, three_recv,
):
    core, level, rank, up, down, sibling = line_of()
    length, width = whole.shape[1:]
    half = length // 2
    own_cols = dcol_ref.shape[2]
    count = length // chunk
    reach = taps // 2
    tile = min(512, width)
    place = lax.axis_index("dp")
    x_mate, y_mate = mate_of(place, level, 1), mate_of(place, level, 2)
    b0, b1, b2 = place % 2, place // 2 % 2, place // 4 % 2
    levels = other_ref.shape[3]
    cut = width // 2
    left_half, right_half = slice(0, cut), slice(cut, width)
    greet(rank, 3, up, down, (sibling, x_mate, y_mate))

    def own_load(z):
        return pltpu.make_async_copy(other_ref.at[:, :, b0, z], own_sum.at[z], own_sem.at[z])

    def one_copy(z):
        part = other_ref.at[:, :, 1 - b0, z]
        return remote(part, rx_one.at[z], one_send.at[z], one_recv.at[z], sibling)

    def two_copy(z, k):
        if k == 0:
            part = own_sum.at[z, :, 1 - b1, :, left_half]
        else:
            part = own_sum.at[z, 1 - b2, :, :, right_half]
        sems = (two_send.at[z, k], two_recv.at[z, k])
        return remote(part, rx_two.at[z, k], sems[0], sems[1], (x_mate, y_mate)[k])

    def three_copy(z, k):
        if k == 0:
            part = own_sum.at[z, 1 - b2, b1, :, left_half]
        else:
            part = own_sum.at[z, b2, 1 - b1, :, right_half]
        sems = (three_send.at[z, k], three_recv.at[z, k])
        return remote(part, rx_three.at[z, k], sems[0], sems[1], (y_mate, x_mate)[k])

    def added(left, right):
        return (left.astype(f32) + right.astype(f32)).astype(bf16)

    def other_second(z):
        one_copy(z).wait_recv()
        load = pltpu.make_async_copy(rx_one.at[z], loaded, load_sem)
        load.start()
        own_load(z).wait()
        load.wait()
        own_sum[z] = added(own_sum[z], loaded[...])
        two_copy(z, 0).start()
        two_copy(z, 1).start()

    def other_third(z):
        two_copy(z, 0).wait_recv()
        two_copy(z, 1).wait_recv()
        for b in range(2):
            kept = own_sum[z, b, b1, :, left_half]
            own_sum[z, b, b1, :, left_half] = added(kept, rx_two[z, 0, b])
            kept = own_sum[z, b2, b, :, right_half]
            own_sum[z, b2, b, :, right_half] = added(kept, rx_two[z, 1, b])
        three_copy(z, 0).start()
        three_copy(z, 1).start()

    def other_fourth(z):
        three_copy(z, 0).wait_recv()
        three_copy(z, 1).wait_recv()
        part_ref[z, :, left_half] = added(own_sum[z, b2, b1, :, left_half], rx_three[z, 0])
        part_ref[z, :, right_half] = added(own_sum[z, b2, b1, :, right_half], rx_three[z, 1])

    def far_copy(c):
        rows = pl.ds(c * chunk, chunk)
        part = whole.at[0, rows]
        return remote(part, part, far_send.at[c], far_recv.at[c], up)

    def near_copy(c):
        rows = pl.ds(c * chunk, chunk)
        part = whole.at[1, rows]
        return remote(part, part, near_send.at[c], near_recv.at[c], up)

    def back_copy(c):
        rows = pl.ds(c * chunk, chunk)
        part = whole.at[1, rows]
        return remote(part, part, back_send.at[c], back_recv.at[c], down)

    slot = jnp.where((rank == 0) | (rank == 3), 0, 1)
    mine = whole.at[slot, pl.ds(core * half, half)]
    half_copy = remote(grad_ref, mine, half_send, half_recv, sibling)
    keep_copy = pltpu.make_async_copy(grad_ref, mine, keep_sem)

    @pl.when(rank >= 2)
    def _():
        half_copy.start()

    @pl.when(rank < 2)
    def _():
        keep_copy.start()

    for z in range(levels):
        one_copy(z).start()
        own_load(z).start()
    gsum[...] = jnp.zeros_like(gsum)
    acc[...] = jnp.zeros_like(acc)

    @pl.when(rank >= 2)
    def _():
        half_copy.wait_send()

    @pl.when(rank < 2)
    def _():
        keep_copy.wait()
        half_copy.wait_recv()

    def item(i):
        edge = (i == 0) | (i == 2 * count - 1)
        near = (i == 0) | ((i % 2 == 1) & (i != 2 * count - 1))
        c = jnp.where(edge, jnp.where(near, 0, count - 1), jnp.where(near, (i + 1) // 2, i // 2 - 1))
        return jnp.where(rank == 0, i >= count, near), jnp.where(rank == 0, i % count, c)

    def sent(i):
        near, c = item(i)

        @pl.when(near)
        def _():
            near_copy(c).wait_send()

        @pl.when(jnp.logical_not(near))
        def _():
            far_copy(c).wait_send()

    def step(i, _):
        @pl.when((i >= 1) & (i < 1 + levels))
        def _():
            other_second(i - 1)

        @pl.when((i >= 3) & (i < 3 + levels))
        def _():
            other_third(i - 3)

        @pl.when(i >= 5)
        def _():
            other_fourth(i - 5)

        near, c = item(i)
        seq = jnp.where(near, 1, 0)

        @pl.when(near)
        def _():
            @pl.when(rank >= 2)
            def _():
                near_copy(c).wait_recv()

            @pl.when(rank == 0)
            def _():
                back_copy(c).wait_recv()

        @pl.when(jnp.logical_not(near) & (rank > 0))
        def _():
            far_copy(c).wait_recv()

        @pl.when(((rank == 1) | (rank == 2)) & (i >= 2) | (rank == 0) & (i >= 2) & (i < count))
        def _():
            sent(i - 2)

        @pl.when(near & ((rank == 1) | (rank == 2)))
        def _():
            near_copy(c).start()

        @pl.when(near & (rank == 1))
        def _():
            @pl.when(c >= 2)
            def _():
                back_copy(c - 2).wait_send()

            back_copy(c).start()

        @pl.when(jnp.logical_not(near) & (rank < 3))
        def _():
            far_copy(c).start()

        rows = pl.ds(pl.multiple_of(c * chunk, chunk), chunk)
        grad = whole[seq, rows, :]
        own = pl.ds(pl.multiple_of(level * own_cols, 128), own_cols)
        dcol_ref[seq, rows, :] = whole[seq, rows, own]
        edge_rows = jnp.zeros((8, own_cols), f32)
        total = jnp.zeros((chunk + 16, own_cols), f32)
        for t in range(taps):
            term = dot(grad, w_ref[t * own_cols : (t + 1) * own_cols, :], NT)
            term = jnp.concatenate([edge_rows, term, edge_rows], axis=0)
            total = total + pltpu.roll(term, (t - reach) % (chunk + 16), 0)
        acc[seq, pl.ds(pl.multiple_of(c * chunk, 8), chunk + 16), :] += total
        for t in range(taps):
            left = act_ref[seq, rows, t * own_cols : (t + 1) * own_cols]
            for n in range(width // tile):
                cols = slice(n * tile, (n + 1) * tile)
                gsum[t * own_cols : (t + 1) * own_cols, cols] += dot(left, grad[:, cols], TN)
        return 0

    lax.fori_loop(0, 2 * count, step, 0)
    for z in range(2 * count - 5, levels):
        other_fourth(z)
    dact_out = pltpu.make_async_copy(acc.at[:, 8 : 8 + length], dact_ref, out_sem.at[0])
    dact_out.start()

    @pl.when(rank == 0)
    def _():
        sent(count - 2)
        sent(count - 1)

    @pl.when((rank == 1) | (rank == 2))
    def _():
        sent(2 * count - 2)
        sent(2 * count - 1)

    @pl.when(rank == 1)
    def _():
        back_copy(count - 2).wait_send()
        back_copy(count - 1).wait_send()

    for n in range(2):
        size = min(length, gsum.shape[0] - n * length)
        whole[n, :size] = gsum[n * length : n * length + size].astype(bf16)
        out = pltpu.make_async_copy(
            whole.at[n, :size], gw_ref.at[n * length : n * length + size], out_sem.at[1 + n]
        )
        out.start()
    for z in range(levels):
        one_copy(z).wait_send()
        for k in range(2):
            two_copy(z, k).wait_send()
            three_copy(z, k).wait_send()
    dact_out.wait()
    for n in range(2):
        size = min(length, gsum.shape[0] - n * length)
        pltpu.make_async_copy(
            whole.at[n, :size], gw_ref.at[n * length : n * length + size], out_sem.at[1 + n]
        ).wait()


def conv_back(grad, act_taps, weight, other, taps, chunk):
    seqs, length, depth = act_taps.shape
    width = weight.shape[1]
    own_cols = depth // taps
    count = length // chunk
    cell, levels, share, _ = other.shape
    dma = pltpu.SemaphoreType.DMA
    shape = jax.ShapeDtypeStruct
    return pl.pallas_call(
        functools.partial(conv_back_kernel, chunk, taps),
        in_specs=[any_spec(), whole_spec(), whole_spec(), any_spec()],
        out_specs=[any_spec(), whole_spec(), any_spec(), whole_spec(), any_spec()],
        out_shape=[
            shape((seqs, length, own_cols), f32),
            shape((seqs, length, own_cols), bf16),
            shape((depth, width), bf16),
            shape((levels, share, width), bf16),
            shape((levels, 2, 2, share, width), bf16),
        ],
        scratch_shapes=[
            pltpu.VMEM((seqs, length, width), bf16),
            pltpu.VMEM((depth, width), f32),
            pltpu.VMEM((seqs, length + 16, own_cols), f32),
            pltpu.VMEM((levels, 2, 2, share, width), bf16),
            pltpu.VMEM((2, 2, share, width), bf16),
            pltpu.VMEM((levels, 2, 2, share, width // 2), bf16),
            pltpu.VMEM((levels, 2, share, width // 2), bf16),
            dma(()),
            dma(()),
            dma((count,)),
            dma((count,)),
            dma((count,)),
            dma((count,)),
            dma((count,)),
            dma((count,)),
            dma(()),
            dma((3,)),
            dma((levels,)),
            dma(()),
            dma((levels,)),
            dma((levels,)),
            dma((levels, 2)),
            dma((levels, 2)),
            dma((levels, 2)),
            dma((levels, 2)),
        ],
        compiler_params=pltpu.CompilerParams(
            collective_id=1, has_side_effects=True, vmem_limit_bytes=58 << 20
        ),
    )(grad, act_taps, weight, other.reshape(2, 2, 2, levels, share, width))


def weight_grads_kernel(cell, count, *refs):
    out_ref, total = refs[-2], refs[-1]
    at = 0
    for i in range(count):
        left_ref, right_ref = refs[2 * i], refs[2 * i + 1]
        cols = left_ref.shape[2]
        tile = 256 if cols % 256 == 0 else 128
        for n in range(cols // tile):
            part = slice(n * tile, (n + 1) * tile)
            total[part, :] = dot(left_ref[0, :, part], right_ref[...], TN)
        rows = cols // cell
        for p in range(cell):
            out_ref[p, 0, at : at + rows, :] = total[p * rows : (p + 1) * rows, :].astype(bf16)
        at += rows
    if len(refs) > 2 * count + 2:
        extra_ref = refs[2 * count]
        out_ref[:, 0, at:, :] = extra_ref[:, 0]


def weight_grads(pairs, extra, cell):
    groups = pairs[0][0].shape[0]
    width = pairs[0][1].shape[1]
    rows = sum(left.shape[2] for left, _ in pairs) // cell
    specs, args = [], []
    for left, right in pairs:
        specs += [block_spec(*left.shape[1:]), pl.BlockSpec(right.shape, lambda g: (0, 0))]
        args += [left, right]
    if extra is not None:
        rows += extra.shape[2]
        specs.append(pl.BlockSpec((cell, 1) + extra.shape[2:], lambda g: (0, g, 0, 0)))
        args.append(extra)
    flops = sum(2 * left.size * width for left, _ in pairs)
    return pl.pallas_call(
        functools.partial(weight_grads_kernel, cell, len(pairs)),
        grid=(groups,),
        in_specs=specs,
        out_specs=pl.BlockSpec((cell, 1, rows, width), lambda g: (0, g, 0, 0)),
        out_shape=jax.ShapeDtypeStruct((cell, groups, rows, width), bf16),
        scratch_shapes=[pltpu.VMEM((max(left.shape[2] for left, _ in pairs), width), f32)],
        cost_estimate=pl.CostEstimate(flops=flops, bytes_accessed=30 << 20, transcendentals=0),
        compiler_params=pltpu.CompilerParams(vmem_limit_bytes=50 << 20),
    )(*args)


def last_sums_kernel(
    conv_ref, part_ref, conv_out, whole_out,
    total, rx_core, rx_two, tx_two, rx_three, tx_three, tx_line, rx_line,
    core_send, core_recv, two_send, two_recv, three_send, three_recv,
    back_send, back_recv, right_send, right_recv, left_send, left_recv, gather_send, gather_recv,
):
    place, level = lax.axis_index("dp"), lax.axis_index("mp")
    last = lax.axis_size("mp") - 1
    b0, b1, b2 = place % 2, place // 2 % 2, place // 4 % 2
    own = place % 8
    mates = [
        (place + 1 - 2 * b0, level),
        (place + 2 - 4 * b1, level),
        (place + 4 - 8 * b2, level),
    ]
    above, below = (place, level + 1), (place, level - 1)
    rows, width = conv_ref.shape
    r2, r4, r8 = rows // 2, rows // 4, rows // 8
    cut = width // 2
    halves = (slice(0, cut), slice(cut, width))
    bits = ((b1, b2), (b2, b1))
    across = ((mates[1], mates[2]), (mates[2], mates[1]))

    barrier = pltpu.get_barrier_semaphore()
    for mate in mates:
        pl.semaphore_signal(barrier, inc=1, device_id=mate, device_id_type=MESH)

    @pl.when(level < last)
    def _():
        pl.semaphore_signal(barrier, inc=1, device_id=above, device_id_type=MESH)

    @pl.when(level > 0)
    def _():
        pl.semaphore_signal(barrier, inc=1, device_id=below, device_id_type=MESH)

    pl.semaphore_wait(barrier, jnp.where((level == 0) | (level == last), 4, 5))

    def span(start, size):
        return pl.ds(pl.multiple_of(start, 16), size)

    mine = b0 * r2
    core_copy = remote(
        conv_ref.at[span((1 - b0) * r2, r2)], rx_core, core_send.at[0], core_recv.at[0], mates[0]
    )
    core_copy.start()

    def right(t, src):
        return remote(src, rx_line.at[t], right_send.at[t], right_recv.at[t], above)

    def left(t, src):
        slot = jnp.where(level - 1 == t, last + 1, t)
        return remote(src, rx_line.at[slot], left_send.at[t], left_recv.at[t], below)

    @pl.when(level == 0)
    def _():
        for t in range(last, 0, -1):
            right(t, part_ref.at[t]).start()

    @pl.when(level == last)
    def _():
        for t in range(last):
            left(t, part_ref.at[t]).start()

    def add_line(t):
        tx_line[t] = (part_ref[t].astype(f32) + rx_line[t].astype(f32)).astype(bf16)

    def pass_right(t, at):
        @pl.when(level == at)
        def _():
            right(t, part_ref.at[t]).wait_recv()
            add_line(t)
            right(t, tx_line.at[t]).start()

    def pass_left(t, at):
        @pl.when(level == at)
        def _():
            left(t, part_ref.at[t]).wait_recv()
            add_line(t)
            left(t, tx_line.at[t]).start()

    core_copy.wait_recv()
    total[...] = conv_ref[span(mine, r2), :].astype(f32) + rx_core[...].astype(f32)
    copies = []
    for h in range(2):
        first = bits[h][0]
        tx_two[h] = total[span((1 - first) * r4, r4), halves[h]].astype(bf16)
        copies.append(
            remote(tx_two.at[h], rx_two.at[h], two_send.at[h], two_recv.at[h], across[h][0])
        )
        copies[h].start()

    pass_right(3, 1)
    pass_left(0, 2)

    deeper = []
    for h in range(2):
        first, second = bits[h]
        copies[h].wait_recv()
        total[span(first * r4, r4), halves[h]] += rx_two[h].astype(f32)
        tx_three[h] = total[span(first * r4 + (1 - second) * r8, r8), halves[h]].astype(bf16)
        deeper.append(
            remote(
                tx_three.at[h], rx_three.at[h], three_send.at[h], three_recv.at[h], across[h][1]
            )
        )
        deeper[h].start()

    pass_right(3, 2)
    pass_left(0, 1)
    pass_right(2, 1)
    pass_left(1, 2)

    def back_copy(h, start, size, stage, mate):
        part = conv_out.at[span(start, size), halves[h]]
        return remote(part, part, back_send.at[stage, h], back_recv.at[stage, h], mate)

    stage_one, stage_two = [], []
    for h in range(2):
        first, second = bits[h]
        deeper[h].wait_recv()
        at = first * r4 + second * r8
        block = total[span(at, r8), halves[h]] + rx_three[h].astype(f32)
        conv_out[span(mine + at, r8), halves[h]] = block.astype(bf16)
        stage_one.append(back_copy(h, mine + at, r8, 0, across[h][1]))
        stage_one[h].start()
    for h in range(2):
        first = bits[h][0]
        stage_one[h].wait_recv()
        stage_two.append(back_copy(h, mine + first * r4, r4, 1, across[h][0]))
        stage_two[h].start()

    for t in range(last + 1):
        @pl.when(level == t)
        def _(t=t):
            block = part_ref[t].astype(f32)
            if t > 0:
                right(t, part_ref.at[t]).wait_recv()
                block = block + rx_line[t].astype(f32)
            if t < last:
                left(t, part_ref.at[t]).wait_recv()
                block = block + rx_line[last + 1].astype(f32)
            whole_out[own] = block.astype(bf16)

    def gather_copy(block, h, stage, mate):
        part = whole_out.at[block, :, halves[h]]
        k = 3 * h + stage
        return remote(part, part, gather_send.at[k], gather_recv.at[k], mate)

    one = own + 4 - 8 * b2, own + 2 - 4 * b1
    first_copies = [gather_copy(own, 0, 0, mates[2]), gather_copy(own, 1, 0, mates[1])]
    own_copies = [gather_copy(own, 0, 1, mates[1]), gather_copy(own, 1, 1, mates[2])]
    far_copies = [gather_copy(one[0], 0, 2, mates[1]), gather_copy(one[1], 1, 2, mates[2])]
    for h in range(2):
        first_copies[h].start()
        own_copies[h].start()

    for h in range(2):
        stage_two[h].wait_recv()
    region = conv_out.at[span(mine, r2)]
    core_back = remote(region, region, core_send.at[1], core_recv.at[1], mates[0])
    core_back.start()

    for h in range(2):
        first_copies[h].wait_recv()
        far_copies[h].start()

    def mate_copy(j, block):
        part = whole_out.at[block]
        return remote(part, part, gather_send.at[6 + j], gather_recv.at[6 + j], mates[0])

    blocks = [own, own + 2 - 4 * b1, own + 4 - 8 * b2, own + 6 - 4 * b1 - 8 * b2]
    mate_copies = [mate_copy(j, block) for j, block in enumerate(blocks)]
    mate_copies[0].start()
    for h in range(2):
        own_copies[h].wait_recv()
    mate_copies[1].start()
    mate_copies[2].start()
    for h in range(2):
        far_copies[h].wait_recv()
    mate_copies[3].start()

    core_copy.wait_send()
    core_back.wait()
    for j in range(4):
        mate_copies[j].wait()
    for h in range(2):
        copies[h].wait_send()
        deeper[h].wait_send()
        stage_one[h].wait_send()
        stage_two[h].wait_send()
        first_copies[h].wait_send()
        own_copies[h].wait_send()
        far_copies[h].wait_send()
    for t in range(last + 1):
        @pl.when(level < t)
        def _(t=t):
            right(t, part_ref.at[t]).wait_send()

        @pl.when(level > t)
        def _(t=t):
            left(t, part_ref.at[t]).wait_send()


def last_sums(conv, parts):
    rows, width = conv.shape
    levels, share, _ = parts.shape
    cut = width // 2
    dma = pltpu.SemaphoreType.DMA
    return pl.pallas_call(
        last_sums_kernel,
        in_specs=[whole_spec()] * 2,
        out_specs=[whole_spec()] * 2,
        out_shape=[
            jax.ShapeDtypeStruct((rows, width), bf16),
            jax.ShapeDtypeStruct((8, share, width), bf16),
        ],
        scratch_shapes=[
            pltpu.VMEM((rows // 2, width), f32),
            pltpu.VMEM((rows // 2, width), bf16),
            pltpu.VMEM((2, rows // 4, cut), bf16),
            pltpu.VMEM((2, rows // 4, cut), bf16),
            pltpu.VMEM((2, rows // 8, cut), bf16),
            pltpu.VMEM((2, rows // 8, cut), bf16),
            pltpu.VMEM((levels, share, width), bf16),
            pltpu.VMEM((levels + 1, share, width), bf16),
            dma((2,)),
            dma((2,)),
            dma((2,)),
            dma((2,)),
            dma((2,)),
            dma((2,)),
            dma((2, 2)),
            dma((2, 2)),
            dma((levels,)),
            dma((levels,)),
            dma((levels,)),
            dma((levels,)),
            dma((10,)),
            dma((10,)),
        ],
        compiler_params=pltpu.CompilerParams(
            collective_id=2, has_side_effects=True, vmem_limit_bytes=56 << 20
        ),
    )(conv, parts)


def on_device(
    block_input,
    row_order,
    conv_weight,
    batch_gain,
    batch_bias,
    first_gain,
    first_bias,
    w_query,
    w_key,
    w_value,
    relative_weight,
    content_bias,
    position_bias,
    w_out,
    second_gain,
    second_bias,
    w_inner,
    inner_bias,
    w_outer,
    cotangent,
):
    seq_count, length = row_order.shape
    group_rows = seq_count * length
    own_cols = block_input.shape[1]
    taps, _, width = conv_weight.shape
    reach = taps // 2
    pair, dk = content_bias.shape
    dv = w_value.shape[1] // pair
    qcols, vcols = pair * dk, pair * dv
    hidden_cols = w_inner.shape[1]
    features = relative_weight.shape[0]
    depth = lax.axis_size("mp")
    spread = lax.axis_size("dp")
    bits = spread.bit_length() - 1
    assert depth == 4 and seq_count == 2 and spread == 1 << bits and bits > 0
    place, level = lax.axis_index("dp"), lax.axis_index("mp")
    core = place % 2
    total_rows = group_rows * spread
    scale = dk ** (-0.5)
    half = length // 2


    def permute(value, route):
        pairs = []
        for d in range(spread):
            for z in range(depth):
                to = route(d, z)
                if to is not None:
                    pairs.append((d * depth + z, to[0] * depth + to[1]))
        return lax.ppermute(value, AXES, pairs)

    def swap_bit(value, bit):
        return permute(value, lambda d, z: (d ^ (1 << bit), z))

    def sum_dp(value):
        for bit in range(bits):
            value = value + swap_bit(value, bit)
        return value

    cell = min(8, spread)
    assert cell == 8
    cells = spread // cell
    inside = outside = None
    if cells > 1:
        inside = [[c * cell + i for i in range(cell)] for c in range(cells)]
        outside = [[c * cell + i for c in range(cells)] for i in range(cell)]

    def scatter_cell(value):
        value = lax.psum_scatter(value, "dp", scatter_dimension=0, axis_index_groups=inside)
        return value if cells == 1 else lax.psum(value, "dp", axis_index_groups=outside)

    order = row_order + length * jnp.arange(seq_count, dtype=jnp.int32)[:, None]
    order = jnp.concatenate([order, order], axis=0)
    source = lax.dynamic_slice_in_dim(order, core, seq_count, 0).reshape(group_rows)
    rows = block_input[source].reshape(seq_count, length, own_cols)

    local = ((w_inner, 1), (w_outer, 0), (w_out, 0), (w_query, 1), (w_key, 1), (w_value, 1))
    local_rows = sum(value.shape[axis] for value, axis in local)
    share_rows = local_rows // cell

    def share_of(p):
        first, last, at, parts = p * share_rows, (p + 1) * share_rows, 0, []
        for k, (value, axis) in enumerate(local):
            low, high = max(first - at, 0), min(last - at, value.shape[axis])
            at += value.shape[axis]
            if low < high:
                parts.append((k, axis, low, high))

        def build(*values):
            found = []
            for k, axis, low, high in parts:
                part = lax.slice_in_dim(values[k], low, high, axis=axis)
                found.append(part.T if axis else part)
            return jnp.concatenate(found, axis=0)

        return build

    share = lax.switch(
        place % cell, [share_of(p) for p in range(cell)], *(value for value, _ in local)
    )
    small = jnp.concatenate(
        [
            relative_weight.astype(f32),
            content_bias.reshape(1, qcols),
            position_bias.reshape(1, qcols),
            inner_bias.reshape(-1, qcols),
        ],
        axis=0,
    )
    conv_flat = conv_weight.reshape(taps * own_cols, width)
    resid_one, act_taps, stats, small, cot, weights = front(
        rows,
        jnp.stack([batch_gain, batch_bias]),
        conv_flat,
        share,
        small,
        cotangent.reshape(seq_count, 2, half, width),
        taps,
        bits,
        total_rows,
        min(256, half),
    )
    inner_weight = weights[:, :hidden_cols]
    outer_weight = weights[:, hidden_cols : 2 * hidden_cols]
    out_weight = weights[:, 2 * hidden_cols : 2 * hidden_cols + vcols]
    qkv_weight = weights[:, 2 * hidden_cols + vcols :]
    batch_mean, batch_scale = stats[0], stats[1]

    rel_weight = small[:, :features].astype(bf16)
    content_all = small[:, features][:, None, :]
    position_all = small[:, features + 1][:, None, :]
    inner_bias_all = small[:, features + 2 :].reshape(depth, 1, hidden_cols)
    basis = relative_basis(length, features)
    basis = jnp.where(jnp.arange(2 * length)[:, None] < 2 * length - 1, basis, 0.0).astype(bf16)
    basis = lax.dynamic_slice_in_dim(basis, half * (1 - core), length + half, 0)
    rel_keys = jnp.einsum(
        "wf,zfq->zwq", basis, rel_weight, preferred_element_type=f32
    ).astype(bf16)

    normed_one, unit_one, inverse_one = norm_rows(resid_one, first_gain, first_bias)
    normed_one = normed_one.astype(bf16)
    qkv = jnp.einsum("rd,znd->zrn", normed_one, qkv_weight, preferred_element_type=f32)
    query = qkv[:, :, :qcols] * scale
    query_w = (query + content_all).astype(bf16)
    query_r = (query + position_all).astype(bf16)
    kv_own = qkv[:, :, qcols:].astype(bf16)
    kv_other = swap_bit(kv_own, 0)
    kv = jnp.concatenate(
        [jnp.where(core == 0, kv_own, kv_other), jnp.where(core == 0, kv_other, kv_own)], axis=1
    )
    bq = min(256, half)
    attended, prob = attend(query_w, query_r, kv, rel_keys, dk, dv, bq)
    resid_two = resid_one + jnp.einsum(
        "zrn,znd->rd", attended, out_weight, preferred_element_type=f32
    )
    normed_two, unit_two, inverse_two = norm_rows(resid_two, second_gain, second_bias)
    normed_two = normed_two.astype(bf16)
    inner = (
        jnp.einsum("rd,znd->zrn", normed_two, inner_weight, preferred_element_type=f32)
        + inner_bias_all
    )
    hidden = gelu(inner).astype(bf16)
    block_output = (
        resid_two + jnp.einsum("zrn,znd->rd", hidden, outer_weight, preferred_element_type=f32)
    ).astype(bf16)
    block_output = permute(
        block_output, lambda d, z: (d - d % 2 + z // 2, 2 * (z % 2) + d % 2)
    )

    d_hidden = jnp.einsum("rd,znd->zrn", cot, outer_weight, preferred_element_type=f32)
    d_inner32 = d_hidden * gelu_slope(inner)
    d_inner = d_inner32.astype(bf16)
    g_inner_bias = jnp.sum(d_inner.astype(f32), axis=1)
    d_norm_two = jnp.einsum("zrn,znd->rd", d_inner, inner_weight, preferred_element_type=f32)
    feed_grads = weight_grads([(hidden, cot), (d_inner, normed_two)], None, cell)
    feed_parts = scatter_cell(feed_grads)
    g_second_gain = jnp.sum(d_norm_two * unit_two, axis=0)
    g_second_bias = jnp.sum(d_norm_two, axis=0)
    d_resid_two = cot.astype(f32) + norm_back(d_norm_two, unit_two, inverse_two, second_gain)

    d_two, _ = lax.optimization_barrier((d_resid_two.astype(bf16), feed_grads))
    d_attended = jnp.einsum("rd,znd->zrn", d_two, out_weight, preferred_element_type=f32)
    d_attended = d_attended.astype(bf16)
    d_query, query_sums, d_kv, d_rel = attend_back(
        query_w, query_r, kv, rel_keys, prob, d_attended, dk, dv, bq, scale
    )
    d_kv_give = lax.dynamic_slice_in_dim(d_kv, (1 - core) * half, half, 1)
    d_kv_keep = lax.dynamic_slice_in_dim(d_kv, core * half, half, 1)
    d_kv_own = (d_kv_keep.astype(f32) + swap_bit(d_kv_give, 0).astype(f32)).astype(bf16)
    d_qkv = jnp.concatenate([d_query, d_kv_own], axis=2)
    d_norm_one = jnp.einsum("zrn,znd->rd", d_qkv, qkv_weight, preferred_element_type=f32)
    g_first_gain = jnp.sum(d_norm_one * unit_one, axis=0)
    g_first_bias = jnp.sum(d_norm_one, axis=0)
    d_resid_one = (
        d_resid_two + norm_back(d_norm_one, unit_one, inverse_one, first_gain)
    ).astype(bf16)

    g_relative = jnp.einsum("wf,zwq->zfq", basis, d_rel, preferred_element_type=f32)
    of_level = jnp.concatenate(
        [
            g_relative.reshape(depth, -1),
            query_sums[:, 0],
            query_sums[:, 1],
            g_inner_bias,
        ],
        axis=1,
    )
    of_all = jnp.concatenate([g_first_gain, g_first_bias, g_second_gain, g_second_bias])
    of_all = jnp.broadcast_to(of_all[None], (depth, 4 * width))
    extra = jnp.concatenate([of_all, of_level], axis=1)
    used = extra.shape[1]
    extra_rows = -(-used // (cell * width))
    extra = jnp.pad(extra, ((0, 0), (0, extra_rows * cell * width - used)))
    extra = jnp.swapaxes(extra.reshape(depth, cell, extra_rows, width), 0, 1)
    extra = jnp.pad(extra, ((0, 0), (0, 0), (0, -extra_rows % 16), (0, 0))).astype(bf16)
    attend_grads = weight_grads([(attended, d_two), (d_qkv, normed_one)], extra, cell)

    d_act, d_cols, g_conv, attend_parts, _ = conv_back(
        d_resid_one, act_taps, conv_flat, attend_grads, taps, min(256, half)
    )
    d_act = d_act.reshape(group_rows, own_cols)
    centred = (rows.reshape(group_rows, own_cols).astype(f32) - batch_mean) * batch_scale
    pre_act = batch_gain * centred + batch_bias
    d_pre = d_act * gelu_slope(pre_act)
    batch_sums = sum_dp(jnp.stack([jnp.sum(d_pre * centred, axis=0), jnp.sum(d_pre, axis=0)]))
    g_batch_gain, g_batch_bias = batch_sums[0], batch_sums[1]
    d_shifted = d_cols.reshape(group_rows, own_cols).astype(f32)
    d_shifted = d_shifted + batch_gain * batch_scale * (
        d_pre - g_batch_bias / total_rows - centred * g_batch_gain / total_rows
    )
    grad_input = jnp.zeros((group_rows, own_cols), f32).at[source].set(d_shifted)

    if cells > 1:
        attend_parts = lax.psum(attend_parts, "dp", axis_index_groups=outside)
        g_conv = lax.psum(g_conv, "dp", axis_index_groups=outside)
    parts = jnp.concatenate([feed_parts, attend_parts], axis=1)
    g_conv, whole = last_sums(g_conv, parts)
    g_conv = g_conv.astype(f32).reshape(taps, own_cols, width)
    whole = whole.astype(f32)
    sums, at = [], 0
    for cols in (hidden_cols, hidden_cols, vcols, 2 * qcols + vcols):
        sums.append(whole[:, at : at + cols // cell].reshape(cols, width))
        at += cols // cell
    g_outer, g_inner, g_out, g_qkv = sums
    rest = whole[:, at : at + extra_rows].reshape(-1)[:used]

    def take(start, size):
        return rest[start : start + size]

    base = 4 * width
    rel_size = features * qcols

    return (
        block_output,
        grad_input,
        g_conv,
        g_batch_gain,
        g_batch_bias,
        take(0, width),
        take(width, width),
        g_qkv[:qcols].T,
        g_qkv[qcols : 2 * qcols].T,
        g_qkv[2 * qcols :].T,
        take(base, rel_size).reshape(features, qcols),
        take(base + rel_size, qcols).reshape(pair, dk),
        take(base + rel_size + qcols, qcols).reshape(pair, dk),
        g_out,
        take(2 * width, width),
        take(3 * width, width),
        g_inner.T,
        take(base + rel_size + 2 * qcols, hidden_cols),
        g_outer,
    )


def solution(mesh):
    return jax.shard_map(
        on_device,
        mesh=mesh,
        in_specs=(
            P("dp", "mp"),
            P("dp", None),
            P(None, "mp", None),
            P("mp"),
            P("mp"),
            P(),
            P(),
            P(None, "mp"),
            P(None, "mp"),
            P(None, "mp"),
            P(None, "mp"),
            P("mp", None),
            P("mp", None),
            P("mp", None),
            P(),
            P(),
            P(None, "mp"),
            P("mp"),
            P("mp", None),
            P("dp", None),
        ),
        out_specs=(
            P(("dp", "mp"), None),
            P("dp", "mp"),
            P(None, "mp", None),
            P("mp"),
            P("mp"),
            P(),
            P(),
            P(None, "mp"),
            P(None, "mp"),
            P(None, "mp"),
            P(None, "mp"),
            P("mp", None),
            P("mp", None),
            P("mp", None),
            P(),
            P(),
            P(None, "mp"),
            P("mp"),
            P("mp", None),
        ),
        check_vma=False,
    )
```

```python
import functools
import math

import jax
import jax.numpy as jnp
from jax import lax
from jax.experimental import pallas as pl
from jax.experimental.pallas import tpu as pltpu
from jax.sharding import PartitionSpec as P

EPSILON = 1e-05
f32 = jnp.float32
bf16 = jnp.bfloat16
AXES = ("dp", "mp")
MESH = pl.DeviceIdType.MESH
NT = (((1,), (1,)), ((), ()))
TN = (((0,), (0,)), ((), ()))
NN = (((1,), (0,)), ((), ()))


def dot(a, b, dims=NN):
    return lax.dot_general(a, b, dims, preferred_element_type=f32)


def gelu(value):
    return value * jax.nn.sigmoid(1.702 * value)


def gelu_slope(value):
    sig = jax.nn.sigmoid(1.702 * value)
    return sig + 1.702 * value * sig * (1.0 - sig)


def norm_rows(rows, gain, bias):
    centre = rows - jnp.mean(rows, axis=-1, keepdims=True)
    spread = jnp.mean(centre * centre, axis=-1, keepdims=True)
    inverse = lax.rsqrt(spread + EPSILON)
    unit = centre * inverse
    return (unit * gain + bias, unit, inverse)


def norm_back(grad, unit, inverse, gain):
    scaled = grad * gain
    return inverse * (
        scaled
        - jnp.mean(scaled, axis=-1, keepdims=True)
        - unit * jnp.mean(scaled * unit, axis=-1, keepdims=True)
    )


def relative_basis(length, features):
    distance = jnp.arange(2 * length, dtype=f32) - (length - 1)
    half = features // 2
    ratio = jnp.arange(half, dtype=f32) / (half - 1)
    life = jnp.power(jnp.float32(length), ratio)
    decay = jnp.exp(-math.log(2.0) * jnp.abs(distance)[:, None] / life[None, :])
    return jnp.concatenate([decay, jnp.sign(distance)[:, None] * decay], axis=1)


def attend_kernel(dk, dv, bq, qw_ref, qr_ref, kv_ref, rel_ref, out_ref, prob_ref):
    rows, length = qw_ref.shape[1], kv_ref.shape[1]
    width = length + bq
    pair = qw_ref.shape[2] // dk
    lane = lax.broadcasted_iota(jnp.int32, (bq, pair * dk), 1) // dk
    keys = kv_ref[0, :, : pair * dk]
    for b in range(rows // bq):
        at = slice(b * bq, (b + 1) * bq)
        lo = rows - (b + 1) * bq
        window = rel_ref[0, lo : lo + width, :]
        qw, qr = qw_ref[0, at, :], qr_ref[0, at, :]
        zero = jnp.zeros_like(qw)
        mixed = []
        for h in range(pair):
            content = dot(jnp.where(lane == h, qw, zero), keys, NT)
            place = dot(jnp.where(lane == h, qr, zero), window, NT)
            place = pltpu.roll(place, width - (bq - 1), 1, stride=1, stride_axis=0)
            logits = content + place[:, :length]
            weights = jnp.exp(logits - jnp.max(logits, axis=1, keepdims=True))
            prob = (weights * (1.0 / jnp.sum(weights, axis=1, keepdims=True))).astype(bf16)
            prob_ref[0, h, at, :] = prob
            values = kv_ref[0, :, pair * dk + h * dv : pair * dk + (h + 1) * dv]
            mixed.append(dot(prob, values).astype(bf16))
        out_ref[0, at, :] = jnp.concatenate(mixed, axis=1)


def block_spec(*shape):
    return pl.BlockSpec((1,) + shape, lambda g: (g,) + (0,) * len(shape))


def attend(qw, qr, kv, rel, dk, dv, bq):
    groups, rows, qcols = qw.shape
    length, kvcols = kv.shape[1:]
    pair = qcols // dk
    return pl.pallas_call(
        functools.partial(attend_kernel, dk, dv, bq),
        grid=(groups,),
        in_specs=[
            block_spec(rows, qcols),
            block_spec(rows, qcols),
            block_spec(length, kvcols),
            block_spec(rel.shape[1], qcols),
        ],
        out_specs=[block_spec(rows, pair * dv), block_spec(pair, rows, length)],
        out_shape=[
            jax.ShapeDtypeStruct((groups, rows, pair * dv), bf16),
            jax.ShapeDtypeStruct((groups, pair, rows, length), bf16),
        ],
        compiler_params=pltpu.CompilerParams(vmem_limit_bytes=50 << 20),
    )(qw, qr, kv, rel)


def attend_back_kernel(
    dk, dv, bq, scale, qw_ref, qr_ref, kv_ref, rel_ref, prob_ref, dmix_ref,
    dq_ref, sums_ref, dkv_ref, drel_ref, dkt, dvt, drt,
):
    rows, length = qw_ref.shape[1], kv_ref.shape[1]
    width = length + bq
    pair = qw_ref.shape[2] // dk
    qcols = pair * dk
    lane = lax.broadcasted_iota(jnp.int32, (bq, qcols), 1) // dk
    across = lax.broadcasted_iota(jnp.int32, (bq, bq), 0)
    across = across + lax.broadcasted_iota(jnp.int32, (bq, bq), 1)
    flip = jnp.where(across == bq - 1, 1.0, 0.0).astype(bf16)
    keys = kv_ref[0, :, :qcols]
    sums_w = jnp.zeros((1, qcols), f32)
    sums_r = jnp.zeros((1, qcols), f32)
    drt[...] = jnp.zeros_like(drt)
    for b in range(rows // bq):
        at = slice(b * bq, (b + 1) * bq)
        lo = rows - (b + 1) * bq
        window = rel_ref[0, lo : lo + width, :]
        qw, qr = qw_ref[0, at, :], qr_ref[0, at, :]
        zero = jnp.zeros_like(qw)
        qr_flip = dot(flip, qr).astype(bf16)
        dqw = jnp.zeros((bq, qcols), f32)
        dqr = jnp.zeros((bq, qcols), f32)
        for h in range(pair):
            prob = prob_ref[0, h, at, :]
            values = kv_ref[0, :, qcols + h * dv : qcols + (h + 1) * dv]
            dmix = dmix_ref[0, at, h * dv : (h + 1) * dv]
            prob32 = prob.astype(f32)
            part = dot(dmix, values, NT) * prob32
            d_logits = part - prob32 * jnp.sum(part, axis=1, keepdims=True)
            d_logits = d_logits.astype(bf16)
            turned = jnp.concatenate(
                [dot(flip, d_logits), jnp.zeros((bq, width - length), f32)], axis=1
            )
            d_window = pltpu.roll(turned, 0, 1, stride=1, stride_axis=0).astype(bf16)
            dqw = dqw + jnp.where(lane == h, dot(d_logits, keys), 0.0)
            dqr = dqr + jnp.where(lane == h, dot(d_window, window), 0.0)
            key_part = dot(jnp.where(lane == h, qw, zero), d_logits, TN)
            value_part = dot(dmix, prob, TN)
            if b == 0 and h == 0:
                dkt[...] = key_part
            else:
                dkt[...] += key_part
            if b == 0:
                dvt[h] = value_part
            else:
                dvt[h] += value_part
            drt[:, lo : lo + width] += dot(jnp.where(lane == h, qr_flip, zero), d_window, TN)
        high = dqr.astype(bf16)
        dqr = dot(flip, high) + dot(flip, (dqr - high.astype(f32)).astype(bf16))
        sums_w += jnp.sum(dqw, axis=0, keepdims=True)
        sums_r += jnp.sum(dqr, axis=0, keepdims=True)
        dq_ref[0, at, :] = ((dqw + dqr) * scale).astype(bf16)
    sums_ref[0] = jnp.concatenate([sums_w, sums_r, jnp.zeros((6, qcols), f32)], axis=0)
    dkv_ref[0, :, :qcols] = dkt[...].T.astype(bf16)
    for h in range(pair):
        dkv_ref[0, :, qcols + h * dv : qcols + (h + 1) * dv] = dvt[h].T.astype(bf16)
    drel_ref[0] = drt[...].T.astype(bf16)


def attend_back(qw, qr, kv, rel, prob, dmix, dk, dv, bq, scale):
    groups, rows, qcols = qw.shape
    length, kvcols = kv.shape[1:]
    pair = qcols // dk
    rels = rel.shape[1]
    return pl.pallas_call(
        functools.partial(attend_back_kernel, dk, dv, bq, scale),
        grid=(groups,),
        in_specs=[
            block_spec(rows, qcols),
            block_spec(rows, qcols),
            block_spec(length, kvcols),
            block_spec(rels, qcols),
            block_spec(pair, rows, length),
            block_spec(rows, pair * dv),
        ],
        out_specs=[
            block_spec(rows, qcols),
            block_spec(8, qcols),
            block_spec(length, kvcols),
            block_spec(rels, qcols),
        ],
        out_shape=[
            jax.ShapeDtypeStruct((groups, rows, qcols), bf16),
            jax.ShapeDtypeStruct((groups, 8, qcols), f32),
            jax.ShapeDtypeStruct((groups, length, kvcols), bf16),
            jax.ShapeDtypeStruct((groups, rels, qcols), bf16),
        ],
        scratch_shapes=[
            pltpu.VMEM((qcols, length), f32),
            pltpu.VMEM((pair, dv, length), f32),
            pltpu.VMEM((qcols, rels), f32),
        ],
        compiler_params=pltpu.CompilerParams(vmem_limit_bytes=50 << 20),
    )(qw, qr, kv, rel, prob, dmix)


def line_of():
    core, level = lax.axis_index("dp") % 2, lax.axis_index("mp")
    depth = lax.axis_size("mp")
    rank = jnp.where(core == 0, level, depth - 1 - level)
    step = jnp.where(core == 0, 1, -1)
    place = lax.axis_index("dp")
    up, down, sibling = (place, level + step), (place, level - step), (place + 1 - 2 * core, level)
    return core, level, rank, up, down, sibling


def remote(src, dst, send_sem, recv_sem, device):
    return pltpu.make_async_remote_copy(
        src_ref=src,
        dst_ref=dst,
        send_sem=send_sem,
        recv_sem=recv_sem,
        device_id=device,
        device_id_type=MESH,
    )


def greet(rank, last, up, down, mates):
    barrier = pltpu.get_barrier_semaphore()

    @pl.when(rank < last)
    def _():
        pl.semaphore_signal(barrier, inc=1, device_id=up, device_id_type=MESH)

    @pl.when(rank > 0)
    def _():
        pl.semaphore_signal(barrier, inc=1, device_id=down, device_id_type=MESH)

    for mate in mates:
        pl.semaphore_signal(barrier, inc=1, device_id=mate, device_id_type=MESH)
    ends = (rank == 0) | (rank == last)
    pl.semaphore_wait(barrier, jnp.where(ends, 1 + len(mates), 2 + len(mates)))


def mate_of(place, level, bit):
    return place + (1 << bit) - (2 << bit) * (place // (1 << bit) % 2), level


class Both:
    def __init__(self, *copies):
        self.copies = copies

    def start(self):
        for copy in self.copies:
            copy.start()

    def wait_recv(self):
        for copy in self.copies:
            copy.wait_recv()

    def wait_send(self):
        for copy in self.copies:
            copy.wait_send()


def diagonal(size):
    row = lax.broadcasted_iota(jnp.int32, (1, size, size), 1)
    return jnp.where(row == lax.broadcasted_iota(jnp.int32, (1, size, size), 2), 1.0, 0.0)


def encode(rows, whole_ref, step_ref):
    step = jnp.max(jnp.abs(rows), axis=1, keepdims=True) * (1.0 / 32000.0)
    scaled = jnp.round(rows * (1.0 / jnp.maximum(step, 1e-30)))
    whole_ref[...] = scaled.astype(jnp.int32).astype(jnp.int16)
    step = step.reshape(rows.shape[0] // 128, 128, 1)
    step_ref[: step.shape[0], :] = jnp.sum(step * diagonal(128), axis=1)


def decode(whole_ref, step_ref):
    count = whole_ref.shape[0]
    step = step_ref[: count // 128, :].reshape(count // 128, 1, 128)
    step = jnp.sum(step * diagonal(128), axis=2, keepdims=True).reshape(count, 1)
    return whole_ref[...].astype(jnp.int32).astype(f32) * step


def front_kernel(
    chunk, taps, bits, total_rows,
    rows_ref, affine_ref, w_ref, share_ref, small_ref, cot_ref,
    resid_ref, act_ref, stats_ref, small_out, cot_out, weights_ref,
    acc, rx_far, rx_near, rx_back, tx_far, tx_near, stage, rx_half, tx_stats, rx_stats,
    rx_far_step, rx_near_step, rx_back_step, tx_far_step, tx_near_step,
    far_send, far_recv, near_send, near_recv, back_recv, swap_send, swap_recv,
    step_send, step_recv,
    stats_send, stats_recv, small_send, small_recv, cot_send, cot_recv, own_sem,
    up_send, down_send, level_recv, plane_send, plane_recv, cross_send, cross_recv,
    core_send, core_recv,
):
    core, level, rank, up, down, sibling = line_of()
    place = lax.axis_index("dp")
    levels = lax.axis_size("mp")
    own = place % 8
    seqs, length, own_cols = rows_ref.shape
    width = w_ref.shape[1]
    half = length // 2
    reach = taps // 2
    count = length // chunk
    per_half = count // 2
    assert count == 4
    tile = min(512, width)
    cut = width // 2
    mates = [mate_of(place, level, bit) for bit in range(bits)]

    barrier = pltpu.get_barrier_semaphore()
    for r in range(1, 4):
        other = (place, (level + r) % levels)
        pl.semaphore_signal(barrier, inc=1, device_id=other, device_id_type=MESH)
    for mate in mates:
        pl.semaphore_signal(barrier, inc=1, device_id=mate, device_id_type=MESH)

    values = rows_ref[...].astype(f32).reshape(seqs * length, own_cols)
    sums = jnp.sum(values, axis=0, keepdims=True)
    squares = jnp.sum(values * values, axis=0, keepdims=True)
    sums = jnp.concatenate([sums, squares, jnp.zeros((6, own_cols), f32)], axis=0)
    pl.semaphore_wait(barrier, 3 + bits)

    x_mate, y_mate = mates[1], mates[2]
    cross = [own + 2 - 4 * (own // 2 % 2), own + 4 - 8 * (own // 4)]
    corner = cross[0] + cross[1] - own
    left_half, right_half = slice(0, cut), slice(cut, width)

    def piece_at(q):
        base = jnp.where((level == 0) | (level == 3), q, jnp.where(q == 0, 1, jnp.where(q == 1, 0, q)))
        return jnp.where(level < 2, base, 3 - base)

    share_rows = share_ref.shape[0]

    def piece(z, block):
        return weights_ref.at[z, pl.ds(pl.multiple_of(block * share_rows, 16), share_rows)]

    def send(part, sems, device):
        return remote(part, part, sems[0], sems[1], device)

    def up_copy(z):
        return send(piece(z, own), (up_send.at[z], level_recv.at[z]), (place, level + 1))

    def down_copy(z):
        return send(piece(z, own), (down_send.at[z], level_recv.at[z]), (place, level - 1))

    def plane_copy(z, k):
        sems = (plane_send.at[z, k], plane_recv.at[z, k])
        return send(piece(z, own), sems, (x_mate, y_mate)[k])

    def cross_copy(z, k):
        part = piece(z, cross[1 - k]).at[:, (left_half, right_half)[k]]
        return send(part, (cross_send.at[z, k], cross_recv.at[z, k]), (x_mate, y_mate)[k])

    def core_copy(z, k):
        part = piece(z, (own, cross[0], cross[1], corner)[k])
        return send(part, (core_send.at[z, k], core_recv.at[z, k]), sibling)

    def weights_first(q):
        z = piece_at(q)

        @pl.when(z != level)
        def _():
            up_copy(z).wait_recv()

        @pl.when((z <= level) & (level < 3))
        def _():
            up_copy(z).start()

        @pl.when((z >= level) & (level > 0))
        def _():
            down_copy(z).start()

        plane_copy(z, 0).start()
        plane_copy(z, 1).start()
        core_copy(z, 0).start()

    def weights_second(q):
        z = piece_at(q)
        plane_copy(z, 0).wait_recv()
        plane_copy(z, 1).wait_recv()
        cross_copy(z, 0).start()
        cross_copy(z, 1).start()
        core_copy(z, 1).start()
        core_copy(z, 2).start()

    def weights_third(q):
        z = piece_at(q)
        cross_copy(z, 0).wait_recv()
        cross_copy(z, 1).wait_recv()
        core_copy(z, 3).start()

    def weights_fourth(q):
        z = piece_at(q)
        for k in range(4):
            core_copy(z, k).wait_recv()

    stages = (weights_first, weights_second, weights_third, weights_fourth)
    plans = (
        (rank == 0, ((-1, 4, 4, 6), (4, 6, 7, 8), (5, 7, 8, 8), (8, 8, 8, 8))),
        ((rank == 1) | (rank == 2), ((-1, 0, 0, 2), (1, 3, 4, 6), (3, 5, 6, 8), (5, 7, 8, 8))),
        (rank == 3, ((-1, 3, 5, 7), (2, 6, 8, 8), (4, 7, 8, 8), (8, 8, 8, 8))),
    )

    def weights_turn(i):
        for mine, plan in plans:
            for stage, turns in zip(stages, plan):
                for q, turn in enumerate(turns):
                    if isinstance(i, int):
                        if turn == i:
                            pl.when(mine)(functools.partial(stage, q))
                    elif 0 <= turn < 2 * count:
                        pl.when(mine & (i == turn))(functools.partial(stage, q))

    own_copy = pltpu.make_async_copy(share_ref, piece(level, own), own_sem)
    own_copy.start()

    def small_copy(r):
        other = (place, (level + r) % levels)
        sems = (small_send.at[r - 1], small_recv.at[level])
        return remote(small_ref, small_out.at[level], sems[0], sems[1], other)

    for r in range(1, 4):
        small_copy(r).start()
    small_out[level] = small_ref[...]
    cot_copy = remote(cot_ref.at[level % 2, 1 - core], cot_out, cot_send, cot_recv, sibling)
    cot_keep = pltpu.make_async_copy(cot_ref.at[level % 2, core], cot_out, cot_recv)

    @pl.when(rank < 2)
    def _():
        cot_copy.start()
        cot_keep.start()

    own_copy.wait()

    for bit in range(bits):
        tx_stats[bit] = sums
        copy = remote(
            tx_stats.at[bit], rx_stats.at[bit], stats_send.at[bit], stats_recv.at[bit], mates[bit]
        )
        copy.start()
        copy.wait()
        sums = sums + rx_stats[bit]
    weights_first(0)
    mean = sums[0:1] / total_rows
    scale = lax.rsqrt(sums[1:2] / total_rows - mean * mean + EPSILON)
    stats_ref[...] = jnp.concatenate([mean, scale, jnp.zeros((6, own_cols), f32)], axis=0)
    row = lax.broadcasted_iota(jnp.int32, (length, own_cols), 0)
    for seq in range(seqs):
        centred = (rows_ref[seq].astype(f32) - mean) * scale
        act = gelu(affine_ref[0:1, :] * centred + affine_ref[1:2, :])
        for t in range(taps):
            moved = pltpu.roll(act, (reach - t) % length, 0) if t != reach else act
            inside = (row + (t - reach) >= 0) & (row + (t - reach) < length)
            act_ref[seq, :, t * own_cols : (t + 1) * own_cols] = jnp.where(
                inside, moved, 0.0
            ).astype(bf16)

    def line_copy(c, whole, step, sems, k, device):
        rows = pl.ds(pl.multiple_of(c * chunk, chunk), chunk)
        return Both(
            remote(whole[0].at[rows], whole[1].at[rows], sems[0].at[c], sems[1].at[c], device),
            remote(
                step[0].at[c], step[1].at[c], step_send.at[min(k, 1), c], step_recv.at[k, c], device
            ),
        )

    def far_copy(c):
        step = (tx_far_step, rx_far_step)
        return line_copy(c, (tx_far, rx_far), step, (far_send, far_recv), 0, down)

    def near_copy(c):
        step = (tx_near_step, rx_near_step)
        return line_copy(c, (tx_near, rx_near), step, (near_send, near_recv), 1, down)

    def back_copy(c):
        step = (tx_near_step, rx_back_step)
        return line_copy(c, (tx_near, rx_back), step, (near_send, back_recv), 2, up)

    def swap_copy(h):
        rows = pl.ds(h * chunk, chunk)
        return remote(stage.at[rows], rx_half.at[rows], swap_send.at[h], swap_recv.at[h], sibling)

    def finish(c):
        rows = pl.ds(c % per_half * chunk, chunk)

        @pl.when(c // per_half == core)
        def _():
            resid_ref[rows, :] = acc[...]

        @pl.when(c // per_half != core)
        def _():
            stage[rows, :] = acc[...]
            swap_copy(c % per_half).start()

    def step(i, _):
        weights_turn(i)
        c = i % count
        near = jnp.where(rank == 0, i < count, i >= count)
        seq = jnp.where(near, 1, 0)
        rows = pl.ds(pl.multiple_of(c * chunk, chunk), chunk)
        for n in range(width // tile):
            cols = slice(n * tile, (n + 1) * tile)
            acc[:, cols] = dot(act_ref[seq, rows, :], w_ref[:, cols])
        here = pl.ds(pl.multiple_of(level * own_cols, 128), own_cols)
        acc[:, here] += rows_ref[seq, rows, :].astype(f32)

        @pl.when(jnp.logical_not(near))
        def _():
            @pl.when(rank < 3)
            def _():
                far_copy(c).wait_recv()
                acc[...] += decode(rx_far.at[rows], rx_far_step.at[c])

            @pl.when(rank > 0)
            def _():
                encode(acc[...], tx_far.at[rows], tx_far_step.at[c])

                @pl.when(c >= 2)
                def _():
                    far_copy(c - 2).wait_send()

                far_copy(c).start()

            @pl.when(rank == 0)
            def _():
                finish(c)

                @pl.when(c >= 1)
                def _():
                    back_copy(c - 1).wait_send()

                back_copy(c).start()

        @pl.when(near)
        def _():
            @pl.when((rank == 1) | (rank == 2))
            def _():
                near_copy(c).wait_recv()
                acc[...] += decode(rx_near.at[rows], rx_near_step.at[c])

            @pl.when(rank == 1)
            def _():
                back_copy(c).wait_recv()
                acc[...] += decode(rx_back.at[rows], rx_back_step.at[c])
                finish(c)

            @pl.when(rank != 1)
            def _():
                encode(acc[...], tx_near.at[rows], tx_near_step.at[c])

            @pl.when(rank >= 2)
            def _():
                @pl.when(c < 2)
                def _():
                    far_copy(count - 2 + c).wait_send()

                @pl.when(c >= 2)
                def _():
                    near_copy(c - 2).wait_send()

                near_copy(c).start()

        return 0

    lax.fori_loop(0, 2 * count, step, 0)
    weights_turn(2 * count)

    @pl.when(rank >= 2)
    def _():
        def take(h, _):
            rows = pl.ds(pl.multiple_of(h * chunk, chunk), chunk)
            swap_copy(h).wait_recv()
            resid_ref[rows, :] = rx_half[rows, :]
            return 0

        lax.fori_loop(0, per_half, take, 0)
        cot_copy.wait_recv()

    @pl.when(rank < 2)
    def _():
        lax.fori_loop(0, per_half, lambda h, _: (swap_copy(h).wait_send(), 0)[1], 0)
        cot_copy.wait_send()
        cot_keep.wait()

    @pl.when(rank == 1)
    def _():
        far_copy(count - 2).wait_send()
        far_copy(count - 1).wait_send()

    @pl.when(rank >= 2)
    def _():
        near_copy(count - 2).wait_send()
        near_copy(count - 1).wait_send()

    @pl.when(rank == 0)
    def _():
        back_copy(count - 1).wait_send()

    for r in range(1, 4):
        small_copy(r).wait_send()
        other = (level + r) % levels
        part = small_out.at[other]
        remote(part, part, small_send.at[r - 1], small_recv.at[other], sibling).wait_recv()

    def end(z, _):
        @pl.when((z <= level) & (level < 3))
        def _():
            up_copy(z).wait_send()

        @pl.when((z >= level) & (level > 0))
        def _():
            down_copy(z).wait_send()

        for k in range(2):
            plane_copy(z, k).wait_send()
            cross_copy(z, k).wait_send()
        for k in range(4):
            core_copy(z, k).wait_send()
        return 0

    lax.fori_loop(0, levels, end, 0)


def whole_spec():
    return pl.BlockSpec(memory_space=pltpu.VMEM)


def any_spec():
    return pl.BlockSpec(memory_space=pl.ANY)


def front(rows, affine, weight, share, small, cot, taps, bits, total_rows, chunk):
    seqs, length, own_cols = rows.shape
    depth, width = weight.shape
    levels = lax.axis_size("mp")
    half, count = length // 2, length // chunk
    dma = pltpu.SemaphoreType.DMA
    shape = jax.ShapeDtypeStruct
    return pl.pallas_call(
        functools.partial(front_kernel, chunk, taps, bits, total_rows),
        in_specs=[whole_spec()] * 5 + [any_spec()],
        out_specs=[whole_spec()] * 5 + [any_spec()],
        out_shape=[
            shape((half, width), f32),
            shape((seqs, length, depth), bf16),
            shape((8, own_cols), f32),
            shape((levels,) + small.shape, f32),
            shape((half, width), bf16),
            shape((levels, 8 * share.shape[0], width), bf16),
        ],
        scratch_shapes=[
            pltpu.VMEM((chunk, width), f32),
            pltpu.VMEM((length, width), jnp.int16),
            pltpu.VMEM((length, width), jnp.int16),
            pltpu.VMEM((length, width), jnp.int16),
            pltpu.VMEM((length, width), jnp.int16),
            pltpu.VMEM((length, width), jnp.int16),
            pltpu.VMEM((half, width), f32),
            pltpu.VMEM((half, width), f32),
            pltpu.VMEM((bits, 8, own_cols), f32),
            pltpu.VMEM((bits, 8, own_cols), f32),
            pltpu.VMEM((count, 8, 128), f32),
            pltpu.VMEM((count, 8, 128), f32),
            pltpu.VMEM((count, 8, 128), f32),
            pltpu.VMEM((count, 8, 128), f32),
            pltpu.VMEM((count, 8, 128), f32),
            dma((count,)),
            dma((count,)),
            dma((count,)),
            dma((count,)),
            dma((count,)),
            dma((count // 2,)),
            dma((count // 2,)),
            dma((2, count)),
            dma((3, count)),
            dma((bits,)),
            dma((bits,)),
            dma((3,)),
            dma((levels,)),
            dma(()),
            dma(()),
            dma(()),
            dma((levels,)),
            dma((levels,)),
            dma((levels,)),
            dma((levels, 2)),
            dma((levels, 2)),
            dma((levels, 2)),
            dma((levels, 2)),
            dma((levels, 4)),
            dma((levels, 4)),
        ],
        cost_estimate=pl.CostEstimate(
            flops=4 * length * depth * width, bytes_accessed=400 << 20, transcendentals=0
        ),
        compiler_params=pltpu.CompilerParams(
            collective_id=0, has_side_effects=True, vmem_limit_bytes=56 << 20
        ),
    )(rows, affine, weight, share, small, cot)


def conv_back_kernel(
    chunk, taps, grad_ref, act_ref, w_ref, other_ref, dact_ref, dcol_ref, gw_ref, part_ref, rx_one,
    whole, gsum, acc, own_sum, loaded, rx_two, rx_three,
    half_send, half_recv, far_send, far_recv, near_send, near_recv, back_send, back_recv,
    keep_sem, out_sem, own_sem, load_sem, one_send, one_recv, two_send, two_recv, three_send, three_recv,
):
    core, level, rank, up, down, sibling = line_of()
    length, width = whole.shape[1:]
    half = length // 2
    own_cols = dcol_ref.shape[2]
    count = length // chunk
    reach = taps // 2
    tile = min(512, width)
    place = lax.axis_index("dp")
    x_mate, y_mate = mate_of(place, level, 1), mate_of(place, level, 2)
    b0, b1, b2 = place % 2, place // 2 % 2, place // 4 % 2
    levels = other_ref.shape[3]
    cut = width // 2
    left_half, right_half = slice(0, cut), slice(cut, width)
    greet(rank, 3, up, down, (sibling, x_mate, y_mate))

    def own_load(z):
        return pltpu.make_async_copy(other_ref.at[:, :, b0, z], own_sum.at[z], own_sem.at[z])

    def one_copy(z):
        part = other_ref.at[:, :, 1 - b0, z]
        return remote(part, rx_one.at[z], one_send.at[z], one_recv.at[z], sibling)

    def two_copy(z, k):
        if k == 0:
            part = own_sum.at[z, :, 1 - b1, :, left_half]
        else:
            part = own_sum.at[z, 1 - b2, :, :, right_half]
        sems = (two_send.at[z, k], two_recv.at[z, k])
        return remote(part, rx_two.at[z, k], sems[0], sems[1], (x_mate, y_mate)[k])

    def three_copy(z, k):
        if k == 0:
            part = own_sum.at[z, 1 - b2, b1, :, left_half]
        else:
            part = own_sum.at[z, b2, 1 - b1, :, right_half]
        sems = (three_send.at[z, k], three_recv.at[z, k])
        return remote(part, rx_three.at[z, k], sems[0], sems[1], (y_mate, x_mate)[k])

    def added(left, right):
        return (left.astype(f32) + right.astype(f32)).astype(bf16)

    def other_second(z):
        one_copy(z).wait_recv()
        load = pltpu.make_async_copy(rx_one.at[z], loaded, load_sem)
        load.start()
        own_load(z).wait()
        load.wait()
        own_sum[z] = added(own_sum[z], loaded[...])
        two_copy(z, 0).start()
        two_copy(z, 1).start()

    def other_third(z):
        two_copy(z, 0).wait_recv()
        two_copy(z, 1).wait_recv()
        for b in range(2):
            kept = own_sum[z, b, b1, :, left_half]
            own_sum[z, b, b1, :, left_half] = added(kept, rx_two[z, 0, b])
            kept = own_sum[z, b2, b, :, right_half]
            own_sum[z, b2, b, :, right_half] = added(kept, rx_two[z, 1, b])
        three_copy(z, 0).start()
        three_copy(z, 1).start()

    def other_fourth(z):
        three_copy(z, 0).wait_recv()
        three_copy(z, 1).wait_recv()
        part_ref[z, :, left_half] = added(own_sum[z, b2, b1, :, left_half], rx_three[z, 0])
        part_ref[z, :, right_half] = added(own_sum[z, b2, b1, :, right_half], rx_three[z, 1])

    def far_copy(c):
        rows = pl.ds(c * chunk, chunk)
        part = whole.at[0, rows]
        return remote(part, part, far_send.at[c], far_recv.at[c], up)

    def near_copy(c):
        rows = pl.ds(c * chunk, chunk)
        part = whole.at[1, rows]
        return remote(part, part, near_send.at[c], near_recv.at[c], up)

    def back_copy(c):
        rows = pl.ds(c * chunk, chunk)
        part = whole.at[1, rows]
        return remote(part, part, back_send.at[c], back_recv.at[c], down)

    slot = jnp.where((rank == 0) | (rank == 3), 0, 1)
    mine = whole.at[slot, pl.ds(core * half, half)]
    half_copy = remote(grad_ref, mine, half_send, half_recv, sibling)
    keep_copy = pltpu.make_async_copy(grad_ref, mine, keep_sem)

    @pl.when(rank >= 2)
    def _():
        half_copy.start()

    @pl.when(rank < 2)
    def _():
        keep_copy.start()

    for z in range(levels):
        one_copy(z).start()
        own_load(z).start()
    gsum[...] = jnp.zeros_like(gsum)
    acc[...] = jnp.zeros_like(acc)

    @pl.when(rank >= 2)
    def _():
        half_copy.wait_send()

    @pl.when(rank < 2)
    def _():
        keep_copy.wait()
        half_copy.wait_recv()

    def item(i):
        edge = (i == 0) | (i == 2 * count - 1)
        near = (i == 0) | ((i % 2 == 1) & (i != 2 * count - 1))
        c = jnp.where(edge, jnp.where(near, 0, count - 1), jnp.where(near, (i + 1) // 2, i // 2 - 1))
        return jnp.where(rank == 0, i >= count, near), jnp.where(rank == 0, i % count, c)

    def sent(i):
        near, c = item(i)

        @pl.when(near)
        def _():
            near_copy(c).wait_send()

        @pl.when(jnp.logical_not(near))
        def _():
            far_copy(c).wait_send()

    def step(i, _):
        @pl.when((i >= 1) & (i < 1 + levels))
        def _():
            other_second(i - 1)

        @pl.when((i >= 3) & (i < 3 + levels))
        def _():
            other_third(i - 3)

        @pl.when(i >= 5)
        def _():
            other_fourth(i - 5)

        near, c = item(i)
        seq = jnp.where(near, 1, 0)

        @pl.when(near)
        def _():
            @pl.when(rank >= 2)
            def _():
                near_copy(c).wait_recv()

            @pl.when(rank == 0)
            def _():
                back_copy(c).wait_recv()

        @pl.when(jnp.logical_not(near) & (rank > 0))
        def _():
            far_copy(c).wait_recv()

        @pl.when(((rank == 1) | (rank == 2)) & (i >= 2) | (rank == 0) & (i >= 2) & (i < count))
        def _():
            sent(i - 2)

        @pl.when(near & ((rank == 1) | (rank == 2)))
        def _():
            near_copy(c).start()

        @pl.when(near & (rank == 1))
        def _():
            @pl.when(c >= 2)
            def _():
                back_copy(c - 2).wait_send()

            back_copy(c).start()

        @pl.when(jnp.logical_not(near) & (rank < 3))
        def _():
            far_copy(c).start()

        rows = pl.ds(pl.multiple_of(c * chunk, chunk), chunk)
        grad = whole[seq, rows, :]
        own = pl.ds(pl.multiple_of(level * own_cols, 128), own_cols)
        dcol_ref[seq, rows, :] = whole[seq, rows, own]
        edge_rows = jnp.zeros((8, own_cols), f32)
        total = jnp.zeros((chunk + 16, own_cols), f32)
        for t in range(taps):
            term = dot(grad, w_ref[t * own_cols : (t + 1) * own_cols, :], NT)
            term = jnp.concatenate([edge_rows, term, edge_rows], axis=0)
            total = total + pltpu.roll(term, (t - reach) % (chunk + 16), 0)
        acc[seq, pl.ds(pl.multiple_of(c * chunk, 8), chunk + 16), :] += total
        for t in range(taps):
            left = act_ref[seq, rows, t * own_cols : (t + 1) * own_cols]
            for n in range(width // tile):
                cols = slice(n * tile, (n + 1) * tile)
                gsum[t * own_cols : (t + 1) * own_cols, cols] += dot(left, grad[:, cols], TN)
        return 0

    lax.fori_loop(0, 2 * count, step, 0)
    for z in range(2 * count - 5, levels):
        other_fourth(z)
    dact_out = pltpu.make_async_copy(acc.at[:, 8 : 8 + length], dact_ref, out_sem.at[0])
    dact_out.start()

    @pl.when(rank == 0)
    def _():
        sent(count - 2)
        sent(count - 1)

    @pl.when((rank == 1) | (rank == 2))
    def _():
        sent(2 * count - 2)
        sent(2 * count - 1)

    @pl.when(rank == 1)
    def _():
        back_copy(count - 2).wait_send()
        back_copy(count - 1).wait_send()

    for n in range(2):
        size = min(length, gsum.shape[0] - n * length)
        whole[n, :size] = gsum[n * length : n * length + size].astype(bf16)
        out = pltpu.make_async_copy(
            whole.at[n, :size], gw_ref.at[n * length : n * length + size], out_sem.at[1 + n]
        )
        out.start()
    for z in range(levels):
        one_copy(z).wait_send()
        for k in range(2):
            two_copy(z, k).wait_send()
            three_copy(z, k).wait_send()
    dact_out.wait()
    for n in range(2):
        size = min(length, gsum.shape[0] - n * length)
        pltpu.make_async_copy(
            whole.at[n, :size], gw_ref.at[n * length : n * length + size], out_sem.at[1 + n]
        ).wait()


def conv_back(grad, act_taps, weight, other, taps, chunk):
    seqs, length, depth = act_taps.shape
    width = weight.shape[1]
    own_cols = depth // taps
    count = length // chunk
    cell, levels, share, _ = other.shape
    dma = pltpu.SemaphoreType.DMA
    shape = jax.ShapeDtypeStruct
    return pl.pallas_call(
        functools.partial(conv_back_kernel, chunk, taps),
        in_specs=[any_spec(), whole_spec(), whole_spec(), any_spec()],
        out_specs=[any_spec(), whole_spec(), any_spec(), whole_spec(), any_spec()],
        out_shape=[
            shape((seqs, length, own_cols), f32),
            shape((seqs, length, own_cols), bf16),
            shape((depth, width), bf16),
            shape((levels, share, width), bf16),
            shape((levels, 2, 2, share, width), bf16),
        ],
        scratch_shapes=[
            pltpu.VMEM((seqs, length, width), bf16),
            pltpu.VMEM((depth, width), f32),
            pltpu.VMEM((seqs, length + 16, own_cols), f32),
            pltpu.VMEM((levels, 2, 2, share, width), bf16),
            pltpu.VMEM((2, 2, share, width), bf16),
            pltpu.VMEM((levels, 2, 2, share, width // 2), bf16),
            pltpu.VMEM((levels, 2, share, width // 2), bf16),
            dma(()),
            dma(()),
            dma((count,)),
            dma((count,)),
            dma((count,)),
            dma((count,)),
            dma((count,)),
            dma((count,)),
            dma(()),
            dma((3,)),
            dma((levels,)),
            dma(()),
            dma((levels,)),
            dma((levels,)),
            dma((levels, 2)),
            dma((levels, 2)),
            dma((levels, 2)),
            dma((levels, 2)),
        ],
        compiler_params=pltpu.CompilerParams(
            collective_id=1, has_side_effects=True, vmem_limit_bytes=58 << 20
        ),
    )(grad, act_taps, weight, other.reshape(2, 2, 2, levels, share, width))


def weight_grads_kernel(cell, count, *refs):
    out_ref, total = refs[-2], refs[-1]
    at = 0
    for i in range(count):
        left_ref, right_ref = refs[2 * i], refs[2 * i + 1]
        cols = left_ref.shape[2]
        tile = 256 if cols % 256 == 0 else 128
        for n in range(cols // tile):
            part = slice(n * tile, (n + 1) * tile)
            total[part, :] = dot(left_ref[0, :, part], right_ref[...], TN)
        rows = cols // cell
        for p in range(cell):
            out_ref[p, 0, at : at + rows, :] = total[p * rows : (p + 1) * rows, :].astype(bf16)
        at += rows
    if len(refs) > 2 * count + 2:
        extra_ref = refs[2 * count]
        out_ref[:, 0, at:, :] = extra_ref[:, 0]


def weight_grads(pairs, extra, cell):
    groups = pairs[0][0].shape[0]
    width = pairs[0][1].shape[1]
    rows = sum(left.shape[2] for left, _ in pairs) // cell
    specs, args = [], []
    for left, right in pairs:
        specs += [block_spec(*left.shape[1:]), pl.BlockSpec(right.shape, lambda g: (0, 0))]
        args += [left, right]
    if extra is not None:
        rows += extra.shape[2]
        specs.append(pl.BlockSpec((cell, 1) + extra.shape[2:], lambda g: (0, g, 0, 0)))
        args.append(extra)
    flops = sum(2 * left.size * width for left, _ in pairs)
    return pl.pallas_call(
        functools.partial(weight_grads_kernel, cell, len(pairs)),
        grid=(groups,),
        in_specs=specs,
        out_specs=pl.BlockSpec((cell, 1, rows, width), lambda g: (0, g, 0, 0)),
        out_shape=jax.ShapeDtypeStruct((cell, groups, rows, width), bf16),
        scratch_shapes=[pltpu.VMEM((max(left.shape[2] for left, _ in pairs), width), f32)],
        cost_estimate=pl.CostEstimate(flops=flops, bytes_accessed=30 << 20, transcendentals=0),
        compiler_params=pltpu.CompilerParams(vmem_limit_bytes=50 << 20),
    )(*args)


def last_sums_kernel(
    conv_ref, part_ref, conv_out, whole_out,
    total, rx_core, rx_two, tx_two, rx_three, tx_three, tx_line, rx_line,
    core_send, core_recv, two_send, two_recv, three_send, three_recv,
    back_send, back_recv, right_send, right_recv, left_send, left_recv, gather_send, gather_recv,
):
    place, level = lax.axis_index("dp"), lax.axis_index("mp")
    last = lax.axis_size("mp") - 1
    b0, b1, b2 = place % 2, place // 2 % 2, place // 4 % 2
    own = place % 8
    mates = [
        (place + 1 - 2 * b0, level),
        (place + 2 - 4 * b1, level),
        (place + 4 - 8 * b2, level),
    ]
    above, below = (place, level + 1), (place, level - 1)
    rows, width = conv_ref.shape
    r2, r4, r8 = rows // 2, rows // 4, rows // 8
    cut = width // 2
    halves = (slice(0, cut), slice(cut, width))
    bits = ((b1, b2), (b2, b1))
    across = ((mates[1], mates[2]), (mates[2], mates[1]))

    barrier = pltpu.get_barrier_semaphore()
    for mate in mates:
        pl.semaphore_signal(barrier, inc=1, device_id=mate, device_id_type=MESH)

    @pl.when(level < last)
    def _():
        pl.semaphore_signal(barrier, inc=1, device_id=above, device_id_type=MESH)

    @pl.when(level > 0)
    def _():
        pl.semaphore_signal(barrier, inc=1, device_id=below, device_id_type=MESH)

    pl.semaphore_wait(barrier, jnp.where((level == 0) | (level == last), 4, 5))

    def span(start, size):
        return pl.ds(pl.multiple_of(start, 16), size)

    mine = b0 * r2
    core_copy = remote(
        conv_ref.at[span((1 - b0) * r2, r2)], rx_core, core_send.at[0], core_recv.at[0], mates[0]
    )
    core_copy.start()

    def right(t, src):
        return remote(src, rx_line.at[t], right_send.at[t], right_recv.at[t], above)

    def left(t, src):
        slot = jnp.where(level - 1 == t, last + 1, t)
        return remote(src, rx_line.at[slot], left_send.at[t], left_recv.at[t], below)

    @pl.when(level == 0)
    def _():
        for t in range(last, 0, -1):
            right(t, part_ref.at[t]).start()

    @pl.when(level == last)
    def _():
        for t in range(last):
            left(t, part_ref.at[t]).start()

    def add_line(t):
        tx_line[t] = (part_ref[t].astype(f32) + rx_line[t].astype(f32)).astype(bf16)

    def pass_right(t, at):
        @pl.when(level == at)
        def _():
            right(t, part_ref.at[t]).wait_recv()
            add_line(t)
            right(t, tx_line.at[t]).start()

    def pass_left(t, at):
        @pl.when(level == at)
        def _():
            left(t, part_ref.at[t]).wait_recv()
            add_line(t)
            left(t, tx_line.at[t]).start()

    core_copy.wait_recv()
    total[...] = conv_ref[span(mine, r2), :].astype(f32) + rx_core[...].astype(f32)
    copies = []
    for h in range(2):
        first = bits[h][0]
        tx_two[h] = total[span((1 - first) * r4, r4), halves[h]].astype(bf16)
        copies.append(
            remote(tx_two.at[h], rx_two.at[h], two_send.at[h], two_recv.at[h], across[h][0])
        )
        copies[h].start()

    pass_right(3, 1)
    pass_left(0, 2)

    deeper = []
    for h in range(2):
        first, second = bits[h]
        copies[h].wait_recv()
        total[span(first * r4, r4), halves[h]] += rx_two[h].astype(f32)
        tx_three[h] = total[span(first * r4 + (1 - second) * r8, r8), halves[h]].astype(bf16)
        deeper.append(
            remote(
                tx_three.at[h], rx_three.at[h], three_send.at[h], three_recv.at[h], across[h][1]
            )
        )
        deeper[h].start()

    pass_right(3, 2)
    pass_left(0, 1)
    pass_right(2, 1)
    pass_left(1, 2)

    def back_copy(h, start, size, stage, mate):
        part = conv_out.at[span(start, size), halves[h]]
        return remote(part, part, back_send.at[stage, h], back_recv.at[stage, h], mate)

    stage_one, stage_two = [], []
    for h in range(2):
        first, second = bits[h]
        deeper[h].wait_recv()
        at = first * r4 + second * r8
        block = total[span(at, r8), halves[h]] + rx_three[h].astype(f32)
        conv_out[span(mine + at, r8), halves[h]] = block.astype(bf16)
        stage_one.append(back_copy(h, mine + at, r8, 0, across[h][1]))
        stage_one[h].start()
    for h in range(2):
        first = bits[h][0]
        stage_one[h].wait_recv()
        stage_two.append(back_copy(h, mine + first * r4, r4, 1, across[h][0]))
        stage_two[h].start()

    for t in range(last + 1):
        @pl.when(level == t)
        def _(t=t):
            block = part_ref[t].astype(f32)
            if t > 0:
                right(t, part_ref.at[t]).wait_recv()
                block = block + rx_line[t].astype(f32)
            if t < last:
                left(t, part_ref.at[t]).wait_recv()
                block = block + rx_line[last + 1].astype(f32)
            whole_out[own] = block.astype(bf16)

    def gather_copy(block, h, stage, mate):
        part = whole_out.at[block, :, halves[h]]
        k = 3 * h + stage
        return remote(part, part, gather_send.at[k], gather_recv.at[k], mate)

    one = own + 4 - 8 * b2, own + 2 - 4 * b1
    first_copies = [gather_copy(own, 0, 0, mates[2]), gather_copy(own, 1, 0, mates[1])]
    own_copies = [gather_copy(own, 0, 1, mates[1]), gather_copy(own, 1, 1, mates[2])]
    far_copies = [gather_copy(one[0], 0, 2, mates[1]), gather_copy(one[1], 1, 2, mates[2])]
    for h in range(2):
        first_copies[h].start()
        own_copies[h].start()

    for h in range(2):
        stage_two[h].wait_recv()
    region = conv_out.at[span(mine, r2)]
    core_back = remote(region, region, core_send.at[1], core_recv.at[1], mates[0])
    core_back.start()

    for h in range(2):
        first_copies[h].wait_recv()
        far_copies[h].start()

    def mate_copy(j, block):
        part = whole_out.at[block]
        return remote(part, part, gather_send.at[6 + j], gather_recv.at[6 + j], mates[0])

    blocks = [own, own + 2 - 4 * b1, own + 4 - 8 * b2, own + 6 - 4 * b1 - 8 * b2]
    mate_copies = [mate_copy(j, block) for j, block in enumerate(blocks)]
    mate_copies[0].start()
    for h in range(2):
        own_copies[h].wait_recv()
    mate_copies[1].start()
    mate_copies[2].start()
    for h in range(2):
        far_copies[h].wait_recv()
    mate_copies[3].start()

    core_copy.wait_send()
    core_back.wait()
    for j in range(4):
        mate_copies[j].wait()
    for h in range(2):
        copies[h].wait_send()
        deeper[h].wait_send()
        stage_one[h].wait_send()
        stage_two[h].wait_send()
        first_copies[h].wait_send()
        own_copies[h].wait_send()
        far_copies[h].wait_send()
    for t in range(last + 1):
        @pl.when(level < t)
        def _(t=t):
            right(t, part_ref.at[t]).wait_send()

        @pl.when(level > t)
        def _(t=t):
            left(t, part_ref.at[t]).wait_send()


def last_sums(conv, parts):
    rows, width = conv.shape
    levels, share, _ = parts.shape
    cut = width // 2
    dma = pltpu.SemaphoreType.DMA
    return pl.pallas_call(
        last_sums_kernel,
        in_specs=[whole_spec()] * 2,
        out_specs=[whole_spec()] * 2,
        out_shape=[
            jax.ShapeDtypeStruct((rows, width), bf16),
            jax.ShapeDtypeStruct((8, share, width), bf16),
        ],
        scratch_shapes=[
            pltpu.VMEM((rows // 2, width), f32),
            pltpu.VMEM((rows // 2, width), bf16),
            pltpu.VMEM((2, rows // 4, cut), bf16),
            pltpu.VMEM((2, rows // 4, cut), bf16),
            pltpu.VMEM((2, rows // 8, cut), bf16),
            pltpu.VMEM((2, rows // 8, cut), bf16),
            pltpu.VMEM((levels, share, width), bf16),
            pltpu.VMEM((levels + 1, share, width), bf16),
            dma((2,)),
            dma((2,)),
            dma((2,)),
            dma((2,)),
            dma((2,)),
            dma((2,)),
            dma((2, 2)),
            dma((2, 2)),
            dma((levels,)),
            dma((levels,)),
            dma((levels,)),
            dma((levels,)),
            dma((10,)),
            dma((10,)),
        ],
        compiler_params=pltpu.CompilerParams(
            collective_id=2, has_side_effects=True, vmem_limit_bytes=56 << 20
        ),
    )(conv, parts)


def give_kernel(
    cuts, conv_ref, part_ref,
    conv_out, outer_out, inner_out, out_out, query_out, key_out, value_out, rest_out,
    inner_rows, qkv_rows,
):
    p = pl.program_id(0)
    cell = pl.num_programs(0)
    conv_out[...] = conv_ref[...].astype(f32)
    a, b, c, d = cuts[0], cuts[0] + cuts[1], sum(cuts[:3]), sum(cuts)
    outer_out[...] = part_ref[0, :a].astype(f32)
    inner_rows[pl.ds(pl.multiple_of(p * cuts[1], 16), cuts[1])] = part_ref[0, a:b]
    out_out[...] = part_ref[0, b:c].astype(f32)
    qkv_rows[pl.ds(pl.multiple_of(p * cuts[3], 16), cuts[3])] = part_ref[0, c:d]
    rest_out[0] = part_ref[0, d:].astype(f32)

    @pl.when(p == cell - 1)
    def _():
        inner_out[...] = inner_rows[...].astype(f32).T
        at = 0
        for out in (query_out, key_out, value_out):
            size = out.shape[1]
            out[...] = qkv_rows[at : at + size].astype(f32).T
            at += size


def give(conv, parts, cuts, qcols, vcols):
    rows, width = conv.shape
    cell, share, _ = parts.shape
    rest = share - sum(cuts)
    shape = jax.ShapeDtypeStruct
    by_rows = lambda size: pl.BlockSpec((size, width), lambda p: (p, 0))
    fixed = lambda cols: pl.BlockSpec((width, cols), lambda p: (0, 0))
    inner_cols = cell * cuts[1]
    return pl.pallas_call(
        functools.partial(give_kernel, cuts),
        grid=(cell,),
        in_specs=[by_rows(rows // cell), block_spec(share, width)],
        out_specs=[
            by_rows(rows // cell),
            by_rows(cuts[0]),
            fixed(inner_cols),
            by_rows(cuts[2]),
            fixed(qcols),
            fixed(qcols),
            fixed(vcols),
            block_spec(rest, width),
        ],
        out_shape=[
            shape((rows, width), f32),
            shape((cell * cuts[0], width), f32),
            shape((width, inner_cols), f32),
            shape((cell * cuts[2], width), f32),
            shape((width, qcols), f32),
            shape((width, qcols), f32),
            shape((width, vcols), f32),
            shape((cell, rest, width), f32),
        ],
        scratch_shapes=[
            pltpu.VMEM((inner_cols, width), bf16),
            pltpu.VMEM((cell * cuts[3], width), bf16),
        ],
        compiler_params=pltpu.CompilerParams(vmem_limit_bytes=50 << 20),
    )(conv, parts)


def on_device(
    block_input,
    row_order,
    conv_weight,
    batch_gain,
    batch_bias,
    first_gain,
    first_bias,
    w_query,
    w_key,
    w_value,
    relative_weight,
    content_bias,
    position_bias,
    w_out,
    second_gain,
    second_bias,
    w_inner,
    inner_bias,
    w_outer,
    cotangent,
):
    seq_count, length = row_order.shape
    group_rows = seq_count * length
    own_cols = block_input.shape[1]
    taps, _, width = conv_weight.shape
    reach = taps // 2
    pair, dk = content_bias.shape
    dv = w_value.shape[1] // pair
    qcols, vcols = pair * dk, pair * dv
    hidden_cols = w_inner.shape[1]
    features = relative_weight.shape[0]
    depth = lax.axis_size("mp")
    spread = lax.axis_size("dp")
    bits = spread.bit_length() - 1
    assert depth == 4 and seq_count == 2 and spread == 1 << bits and bits > 0
    place, level = lax.axis_index("dp"), lax.axis_index("mp")
    core = place % 2
    total_rows = group_rows * spread
    scale = dk ** (-0.5)
    half = length // 2


    def permute(value, route):
        pairs = []
        for d in range(spread):
            for z in range(depth):
                to = route(d, z)
                if to is not None:
                    pairs.append((d * depth + z, to[0] * depth + to[1]))
        return lax.ppermute(value, AXES, pairs)

    def swap_bit(value, bit):
        return permute(value, lambda d, z: (d ^ (1 << bit), z))

    def sum_dp(value):
        for bit in range(bits):
            value = value + swap_bit(value, bit)
        return value

    cell = min(8, spread)
    assert cell == 8
    cells = spread // cell
    inside = outside = None
    if cells > 1:
        inside = [[c * cell + i for i in range(cell)] for c in range(cells)]
        outside = [[c * cell + i for c in range(cells)] for i in range(cell)]

    def scatter_cell(value):
        value = lax.psum_scatter(value, "dp", scatter_dimension=0, axis_index_groups=inside)
        return value if cells == 1 else lax.psum(value, "dp", axis_index_groups=outside)

    order = row_order + length * jnp.arange(seq_count, dtype=jnp.int32)[:, None]
    order = jnp.concatenate([order, order], axis=0)
    source = lax.dynamic_slice_in_dim(order, core, seq_count, 0).reshape(group_rows)
    rows = block_input[source].reshape(seq_count, length, own_cols)

    local = ((w_inner, 1), (w_outer, 0), (w_out, 0), (w_query, 1), (w_key, 1), (w_value, 1))
    local_rows = sum(value.shape[axis] for value, axis in local)
    share_rows = local_rows // cell

    def share_of(p):
        first, last, at, parts = p * share_rows, (p + 1) * share_rows, 0, []
        for k, (value, axis) in enumerate(local):
            low, high = max(first - at, 0), min(last - at, value.shape[axis])
            at += value.shape[axis]
            if low < high:
                parts.append((k, axis, low, high))

        def build(*values):
            found = []
            for k, axis, low, high in parts:
                part = lax.slice_in_dim(values[k], low, high, axis=axis)
                found.append(part.T if axis else part)
            return jnp.concatenate(found, axis=0)

        return build

    share = lax.switch(
        place % cell, [share_of(p) for p in range(cell)], *(value for value, _ in local)
    )
    small = jnp.concatenate(
        [
            relative_weight.astype(f32),
            content_bias.reshape(1, qcols),
            position_bias.reshape(1, qcols),
            inner_bias.reshape(-1, qcols),
        ],
        axis=0,
    )
    conv_flat = conv_weight.reshape(taps * own_cols, width)
    resid_one, act_taps, stats, small, cot, weights = front(
        rows,
        jnp.stack([batch_gain, batch_bias]),
        conv_flat,
        share,
        small,
        cotangent.reshape(seq_count, 2, half, width),
        taps,
        bits,
        total_rows,
        min(256, half),
    )
    inner_weight = weights[:, :hidden_cols]
    outer_weight = weights[:, hidden_cols : 2 * hidden_cols]
    out_weight = weights[:, 2 * hidden_cols : 2 * hidden_cols + vcols]
    qkv_weight = weights[:, 2 * hidden_cols + vcols :]
    batch_mean, batch_scale = stats[0], stats[1]

    rel_weight = small[:, :features].astype(bf16)
    content_all = small[:, features][:, None, :]
    position_all = small[:, features + 1][:, None, :]
    inner_bias_all = small[:, features + 2 :].reshape(depth, 1, hidden_cols)
    basis = relative_basis(length, features)
    basis = jnp.where(jnp.arange(2 * length)[:, None] < 2 * length - 1, basis, 0.0).astype(bf16)
    basis = lax.dynamic_slice_in_dim(basis, half * (1 - core), length + half, 0)
    rel_keys = jnp.einsum(
        "wf,zfq->zwq", basis, rel_weight, preferred_element_type=f32
    ).astype(bf16)

    normed_one, unit_one, inverse_one = norm_rows(resid_one, first_gain, first_bias)
    normed_one = normed_one.astype(bf16)
    qkv = jnp.einsum("rd,znd->zrn", normed_one, qkv_weight, preferred_element_type=f32)
    query = qkv[:, :, :qcols] * scale
    query_w = (query + content_all).astype(bf16)
    query_r = (query + position_all).astype(bf16)
    kv_own = qkv[:, :, qcols:].astype(bf16)
    kv_other = swap_bit(kv_own, 0)
    kv = jnp.concatenate(
        [jnp.where(core == 0, kv_own, kv_other), jnp.where(core == 0, kv_other, kv_own)], axis=1
    )
    bq = min(256, half)
    attended, prob = attend(query_w, query_r, kv, rel_keys, dk, dv, bq)
    resid_two = resid_one + jnp.einsum(
        "zrn,znd->rd", attended, out_weight, preferred_element_type=f32
    )
    normed_two, unit_two, inverse_two = norm_rows(resid_two, second_gain, second_bias)
    normed_two = normed_two.astype(bf16)
    inner = (
        jnp.einsum("rd,znd->zrn", normed_two, inner_weight, preferred_element_type=f32)
        + inner_bias_all
    )
    hidden = gelu(inner).astype(bf16)
    block_output = (
        resid_two + jnp.einsum("zrn,znd->rd", hidden, outer_weight, preferred_element_type=f32)
    ).astype(bf16)
    block_output = permute(
        block_output, lambda d, z: (d - d % 2 + z // 2, 2 * (z % 2) + d % 2)
    )

    d_hidden = jnp.einsum("rd,znd->zrn", cot, outer_weight, preferred_element_type=f32)
    d_inner32 = d_hidden * gelu_slope(inner)
    d_inner = d_inner32.astype(bf16)
    g_inner_bias = jnp.sum(d_inner.astype(f32), axis=1)
    d_norm_two = jnp.einsum("zrn,znd->rd", d_inner, inner_weight, preferred_element_type=f32)
    feed_grads = weight_grads([(hidden, cot), (d_inner, normed_two)], None, cell)
    feed_parts = scatter_cell(feed_grads)
    g_second_gain = jnp.sum(d_norm_two * unit_two, axis=0)
    g_second_bias = jnp.sum(d_norm_two, axis=0)
    d_resid_two = cot.astype(f32) + norm_back(d_norm_two, unit_two, inverse_two, second_gain)

    d_two, _ = lax.optimization_barrier((d_resid_two.astype(bf16), feed_grads))
    d_attended = jnp.einsum("rd,znd->zrn", d_two, out_weight, preferred_element_type=f32)
    d_attended = d_attended.astype(bf16)
    d_query, query_sums, d_kv, d_rel = attend_back(
        query_w, query_r, kv, rel_keys, prob, d_attended, dk, dv, bq, scale
    )
    d_kv_give = lax.dynamic_slice_in_dim(d_kv, (1 - core) * half, half, 1)
    d_kv_keep = lax.dynamic_slice_in_dim(d_kv, core * half, half, 1)
    d_kv_own = (d_kv_keep.astype(f32) + swap_bit(d_kv_give, 0).astype(f32)).astype(bf16)
    d_qkv = jnp.concatenate([d_query, d_kv_own], axis=2)
    d_norm_one = jnp.einsum("zrn,znd->rd", d_qkv, qkv_weight, preferred_element_type=f32)
    g_first_gain = jnp.sum(d_norm_one * unit_one, axis=0)
    g_first_bias = jnp.sum(d_norm_one, axis=0)
    d_resid_one = (
        d_resid_two + norm_back(d_norm_one, unit_one, inverse_one, first_gain)
    ).astype(bf16)

    g_relative = jnp.einsum("wf,zwq->zfq", basis, d_rel, preferred_element_type=f32)
    of_level = jnp.concatenate(
        [
            g_relative.reshape(depth, -1),
            query_sums[:, 0],
            query_sums[:, 1],
            g_inner_bias,
        ],
        axis=1,
    )
    of_all = jnp.concatenate([g_first_gain, g_first_bias, g_second_gain, g_second_bias])
    of_all = jnp.broadcast_to(of_all[None], (depth, 4 * width))
    extra = jnp.concatenate([of_all, of_level], axis=1)
    used = extra.shape[1]
    extra_rows = -(-used // (cell * width))
    extra = jnp.pad(extra, ((0, 0), (0, extra_rows * cell * width - used)))
    extra = jnp.swapaxes(extra.reshape(depth, cell, extra_rows, width), 0, 1)
    extra = jnp.pad(extra, ((0, 0), (0, 0), (0, -extra_rows % 16), (0, 0))).astype(bf16)
    attend_grads = weight_grads([(attended, d_two), (d_qkv, normed_one)], extra, cell)

    d_act, d_cols, g_conv, attend_parts, _ = conv_back(
        d_resid_one, act_taps, conv_flat, attend_grads, taps, min(256, half)
    )
    d_act = d_act.reshape(group_rows, own_cols)
    centred = (rows.reshape(group_rows, own_cols).astype(f32) - batch_mean) * batch_scale
    pre_act = batch_gain * centred + batch_bias
    d_pre = d_act * gelu_slope(pre_act)
    batch_sums = sum_dp(jnp.stack([jnp.sum(d_pre * centred, axis=0), jnp.sum(d_pre, axis=0)]))
    g_batch_gain, g_batch_bias = batch_sums[0], batch_sums[1]
    d_shifted = d_cols.reshape(group_rows, own_cols).astype(f32)
    d_shifted = d_shifted + batch_gain * batch_scale * (
        d_pre - g_batch_bias / total_rows - centred * g_batch_gain / total_rows
    )
    grad_input = jnp.zeros((group_rows, own_cols), f32).at[source].set(d_shifted)

    if cells > 1:
        attend_parts = lax.psum(attend_parts, "dp", axis_index_groups=outside)
        g_conv = lax.psum(g_conv, "dp", axis_index_groups=outside)
    parts = jnp.concatenate([feed_parts, attend_parts], axis=1)
    g_conv, whole = last_sums(g_conv, parts)
    cuts = tuple(
        cols // cell for cols in (hidden_cols, hidden_cols, vcols, 2 * qcols + vcols)
    )
    g_conv, g_outer, g_inner, g_out, g_query, g_key, g_value, rest = give(
        g_conv, whole, cuts, qcols, vcols
    )
    g_conv = g_conv.reshape(taps, own_cols, width)
    rest = rest[:, :extra_rows].reshape(-1)[:used]

    def take(start, size):
        return rest[start : start + size]

    base = 4 * width
    rel_size = features * qcols

    return (
        block_output,
        grad_input,
        g_conv,
        g_batch_gain,
        g_batch_bias,
        take(0, width),
        take(width, width),
        g_query,
        g_key,
        g_value,
        take(base, rel_size).reshape(features, qcols),
        take(base + rel_size, qcols).reshape(pair, dk),
        take(base + rel_size + qcols, qcols).reshape(pair, dk),
        g_out,
        take(2 * width, width),
        take(3 * width, width),
        g_inner,
        take(base + rel_size + 2 * qcols, hidden_cols),
        g_outer,
    )


def solution(mesh):
    return jax.shard_map(
        on_device,
        mesh=mesh,
        in_specs=(
            P("dp", "mp"),
            P("dp", None),
            P(None, "mp", None),
            P("mp"),
            P("mp"),
            P(),
            P(),
            P(None, "mp"),
            P(None, "mp"),
            P(None, "mp"),
            P(None, "mp"),
            P("mp", None),
            P("mp", None),
            P("mp", None),
            P(),
            P(),
            P(None, "mp"),
            P("mp"),
            P("mp", None),
            P("dp", None),
        ),
        out_specs=(
            P(("dp", "mp"), None),
            P("dp", "mp"),
            P(None, "mp", None),
            P("mp"),
            P("mp"),
            P(),
            P(),
            P(None, "mp"),
            P(None, "mp"),
            P(None, "mp"),
            P(None, "mp"),
            P("mp", None),
            P("mp", None),
            P("mp", None),
            P(),
            P(),
            P(None, "mp"),
            P("mp"),
            P("mp", None),
        ),
        check_vma=False,
    )
```
